512 devices in a mesh: expert: 32 (over y, x), dp: 16 (over z, core).
Axes of the slice: x: 4, y: 8, z: 8, core: 2. Of those that a mesh axis runs over, the one named last changes fastest.
Arguments:
- tokens: bfloat16 [2048, 7168], P('expert', 'dp'), may hold values from -6 to 6
- cotangent: bfloat16 [2048, 7168], P('expert', 'dp'), may hold values from -6 to 6
- expert_ids: int32 [2048, 8], P('expert'), may hold values from 0 to 15, all different within a row; in each aligned block of 64 rows (0 to 63, 64 to 127, ...) at most 40 rows name the same one
- route_probs: bfloat16 [2048, 8], P('expert'), may hold values from 0.099609375 to 1
- held_before: int32 [32], replicated, may hold values from 0 to 31, each once
- partner: int32 [32], replicated, may hold values from 0 to 31, as said below
- gate_slabs: bfloat16 [32, 7168, 512], P('expert', 'dp'), may hold values from -0.0625 to 0.0625
- up_slabs: bfloat16 [32, 7168, 512], P('expert', 'dp'), may hold values from -0.0625 to 0.0625
- down_slabs: bfloat16 [32, 512, 7168], P('expert', None, 'dp'), may hold values from -0.1875 to 0.1875
Outputs:
- layer_out: bfloat16 [2048, 7168], P('expert', 'dp')
- token_grad: bfloat16 [2048, 7168], P('expert', 'dp')
- gate_grad: bfloat16 [32, 7168, 512], P('expert', 'dp')
- up_grad: bfloat16 [32, 7168, 512], P('expert', 'dp')
- down_grad: bfloat16 [32, 512, 7168], P('expert', None, 'dp')
The draws below stay inside these ranges and needn't reach their ends.
Inputs may be any that keep to these rules, and one draw needn't show every extreme that they name: `expert_ids`: within the 64 rows of one group (aligned blocks), each row names 8 different experts and no expert is named by more than 40 rows; some expert is named by exactly 40 rows. `held_before`: each slab appears once. partner[partner[j]] == j and partner[j] != j for every j.
All inputs are finite; a program needn't handle non-finite values.
Results may differ from the reference program's by a relative error of at most 0.035.
Values may be sent and summed in bfloat16 or wider, within the bound.
No kernel may reach another device: no remote copies, remote signals or barrier semaphores. Data moves between devices by JAX's collectives and lax.ppermute only.
A program may use at most 64 MiB of HBM per device.

```python
import math
import jax
import jax.numpy as jnp
import numpy as np
from jax import lax

D = 7168
H = 1024
HS = 512
TOK_DEV = 64
CAP = 40
TOKENS = 2048
EXPERTS = 16
TOP_K = 8
N_EXPERT = 32
N_DP = 16


def draw_partner(key, part):
    key = jax.random.fold_in(key, 11)
    shuffled = jax.random.permutation(key, N_EXPERT).astype(jnp.int32)
    first_half = shuffled[0::2]
    second_half = shuffled[1::2]
    result = jnp.zeros((N_EXPERT,), jnp.int32)
    result = result.at[first_half].set(second_half)
    result = result.at[second_half].set(first_half)
    return result


def block_levels(rng, dims, shards, low, largest):
    factor_of, own = 1.0, jax.random.fold_in(rng, 6)
    for axis_at, parts in shards:
        draws = jnp.exp(jax.random.uniform(jax.random.fold_in(own, axis_at), (parts,), jnp.float32, low / len(shards), largest / len(shards)))
        factor_of = factor_of * jnp.repeat(draws, dims[axis_at] // parts).reshape([-1 if axis == axis_at else 1 for axis in range(len(dims))])
    return factor_of


def assign_block(stream_key, own, number, rows, amount, top, most, lean):
    ranking = jax.random.permutation(stream_key, amount)
    packed, usual = shares(amount, rows * top, most, lean, True), shares(amount, rows * top, most, lean, False)
    places = jnp.arange(amount)

    def named(sizes, offset_by):
        used = int((sizes > 0).sum())
        fixed = max(1, used // 4)
        passed = fixed + (places - fixed + offset_by * (used - fixed)) % max(1, amount - fixed)
        return jnp.zeros((amount,), jnp.int32).at[ranking[jnp.where(places < fixed, places, passed)]].set(jnp.asarray(sizes, jnp.int32))

    sizes = jnp.where(number % 4 == 0, named(packed, number // 4), named(usual, number - number // 4 - 1))
    mixed = jax.random.permutation(jax.random.fold_in(own, 3), amount)
    donor, receiver = mixed[0:amount // 2 * 2:2], mixed[1:amount // 2 * 2:2]
    room = jnp.minimum(sizes[donor] - 1, most - sizes[receiver]) // 2
    room = jnp.where((donor == ranking[0]) | (receiver == ranking[0]) | (sizes[receiver] == 0), 0, jnp.maximum(room, 0))
    passed = jax.random.randint(jax.random.fold_in(own, 4), (amount // 2,), 0, 1 << 20) % (room + 1)
    sizes = sizes.at[donor].add(-passed).at[receiver].add(passed)
    items = jnp.searchsorted(jnp.cumsum(sizes), jnp.arange(rows * top), side="right").astype(jnp.int32)
    table = items.reshape(top, rows).T
    table = table[jax.random.permutation(jax.random.fold_in(own, 1), rows)]
    offset_by = jax.random.randint(jax.random.fold_in(own, 2), (rows, 1), 0, top)
    return jnp.take_along_axis(table, (jnp.arange(top)[None, :] + offset_by) % top, axis=1)


def shares(number_of, total, bound, skew, full):
    portions = [(1 << 20) // math.isqrt(rank ** skew) + 1 for rank in range(1, number_of + 1)]
    largest = bound if full else min(bound, max(-(-total // number_of), total * portions[0] // sum(portions)))
    least = 1 if total - largest >= number_of - 1 else 0
    counts, rest = [largest] + [least] * (number_of - 1), total - largest - least * (number_of - 1)
    while rest > 0:
        free = [i for i in range(1, number_of) if counts[i] < largest] or [i for i in range(1, number_of) if counts[i] < bound]
        mass, remaining = sum([portions[i] for i in free]), rest
        for i in free:
            extra = min(bound - counts[i], max(1, remaining * portions[i] // mass), rest)
            counts[i] = counts[i] + extra
            rest = rest - extra
    return np.array(counts)


def bell_draw(rng, shape, scale, reach, pieces=(), kind=jnp.bfloat16):
    array = scale * jax.random.normal(rng, shape, jnp.float32)
    if pieces:
        array = array * block_levels(rng, shape, pieces, -0.22, 0.18)
    return jnp.clip(array, -reach, reach).astype(kind)


def setup_inputs(seed: int = 0) -> dict:
    key_of = jax.random.split(jax.random.key(seed), 10)
    tokens = bell_draw(key_of[0], (TOKENS, D), 1.0, 6.0, ((0, 32), (1, 16)))
    cotangent = bell_draw(key_of[1], (TOKENS, D), 1.0, 6.0, ((0, 32), (1, 16)))
    expert_ids_keys = jax.random.split(jax.random.fold_in(key_of[2], 1), TOKENS // TOK_DEV)
    expert_ids_turns = jax.random.permutation(jax.random.fold_in(key_of[2], 3), TOKENS // TOK_DEV)
    expert_ids = jax.vmap(lambda own, number: assign_block(jax.random.fold_in(key_of[2], 2), own, number, TOK_DEV, EXPERTS, TOP_K, CAP, 2))(expert_ids_keys, expert_ids_turns).reshape((TOKENS, TOP_K))
    route_probs = jnp.clip(0.099609375 + 0.9003906 * jax.random.uniform(key_of[3], (TOKENS, TOP_K), jnp.float32) ** block_levels(key_of[3], (TOKENS, TOP_K), ((0, 32),), -0.2, 0.2), 0.099609375, 1.0).astype(jnp.bfloat16)
    held_before = jax.random.permutation(key_of[4], N_EXPERT).astype(jnp.int32)
    partner = draw_partner(jax.random.fold_in(key_of[9], 71), 0)
    gate_slabs = bell_draw(key_of[6], (N_EXPERT, D, HS), D ** -0.5, 0.0625, ((0, 32), (1, 16)))
    up_slabs = bell_draw(key_of[7], (N_EXPERT, D, HS), D ** -0.5, 0.0625, ((0, 32), (1, 16)))
    down_slabs = bell_draw(key_of[8], (N_EXPERT, HS, D), H ** -0.5, 0.1875, ((0, 32), (2, 16)))
    return {"tokens": tokens, "cotangent": cotangent, "expert_ids": expert_ids, "route_probs": route_probs, "held_before": held_before, "partner": partner, "gate_slabs": gate_slabs, "up_slabs": up_slabs, "down_slabs": down_slabs}


def block_sum(partials):
    rounded = lax.optimization_barrier(partials.astype(jnp.bfloat16))
    return jnp.sum(rounded.astype(jnp.float32), axis=1)


def reference(tokens, cotangent, expert_ids, route_probs, held_before, partner, gate_slabs, up_slabs, down_slabs):
    groups = N_EXPERT
    block_width = D // N_DP
    routing = expert_ids.reshape(groups, TOK_DEV, TOP_K)
    chances = route_probs.reshape(groups, TOK_DEV, TOP_K).astype(jnp.float32)
    slot_iota = lax.broadcasted_iota(jnp.int32, (1, 1, CAP), 2)
    token_index = lax.broadcasted_iota(jnp.int32, (groups, TOK_DEV), 0) * TOK_DEV + lax.broadcasted_iota(jnp.int32, (groups, TOK_DEV), 1)

    def one_slab(running, holder):
        layer_sum, grad_sum = running
        expert = held_before[holder] // 2
        matches = routing == expert
        routed = jnp.sum(matches.astype(jnp.int32), axis=2)
        weights = jnp.sum(jnp.where(matches, chances, jnp.zeros((), jnp.float32)), axis=2)
        position = jnp.cumsum(routed, axis=1) - routed
        select = (routed[:, :, None] == 1) & (position[:, :, None] == slot_iota)
        where_token = jnp.sum(jnp.where(select, token_index[:, :, None], 0), axis=1).reshape(-1).astype(jnp.int32)
        occupied = jnp.any(select, axis=1).reshape(-1, 1)
        slot_probs = jnp.sum(jnp.where(select, weights[:, :, None], jnp.zeros((), jnp.float32)), axis=1).reshape(-1, 1)
        slot_rows = jnp.where(occupied, tokens[where_token], jnp.zeros((), jnp.bfloat16))
        grad_rows = jnp.where(occupied, cotangent[where_token], jnp.zeros((), jnp.bfloat16))
        gate_mat = gate_slabs[holder]
        up_mat = up_slabs[holder]
        down_mat = down_slabs[holder]
        slot_count = slot_rows.shape[0]
        blocked = slot_rows.reshape(slot_count, N_DP, block_width).astype(jnp.float32)
        gate_sum = block_sum(jnp.einsum("rbf,bfh->rbh", blocked, gate_mat.reshape(N_DP, block_width, HS).astype(jnp.float32)))
        up_sum = block_sum(jnp.einsum("rbf,bfh->rbh", blocked, up_mat.reshape(N_DP, block_width, HS).astype(jnp.float32)))
        activated = jax.nn.silu(gate_sum)
        hidden = (activated * up_sum).astype(jnp.bfloat16)
        out_terms = (jnp.dot(hidden, down_mat, preferred_element_type=jnp.float32) * slot_probs).astype(jnp.bfloat16)
        scaled = (slot_probs * grad_rows.astype(jnp.float32)).astype(jnp.bfloat16)
        scaled_blocks = scaled.reshape(slot_count, N_DP, block_width).astype(jnp.float32)
        hidden_grad = block_sum(jnp.einsum("rbf,hbf->rbh", scaled_blocks, down_mat.reshape(HS, N_DP, block_width).astype(jnp.float32)))
        sigmoid_g = jax.nn.sigmoid(gate_sum)
        gate_back = (hidden_grad * up_sum * sigmoid_g * (1.0 + gate_sum * (1.0 - sigmoid_g))).astype(jnp.bfloat16)
        up_back = (hidden_grad * activated).astype(jnp.bfloat16)
        back_terms = (jnp.dot(gate_back, gate_mat.T, preferred_element_type=jnp.float32) + jnp.dot(up_back, up_mat.T, preferred_element_type=jnp.float32)).astype(jnp.bfloat16)
        gate_update = jnp.dot(slot_rows.T, gate_back, preferred_element_type=jnp.float32).astype(jnp.bfloat16)
        up_update = jnp.dot(slot_rows.T, up_back, preferred_element_type=jnp.float32).astype(jnp.bfloat16)
        down_update = jnp.dot(hidden.T, scaled, preferred_element_type=jnp.float32).astype(jnp.bfloat16)
        layer_sum = layer_sum.at[where_token].add(out_terms.astype(jnp.float32))
        grad_sum = grad_sum.at[where_token].add(back_terms.astype(jnp.float32))
        return (layer_sum, grad_sum), (gate_update, up_update, down_update)

    start = (jnp.zeros(tokens.shape, jnp.float32), jnp.zeros(tokens.shape, jnp.float32))
    (layer_sum, grad_sum), (gate_all, up_all, down_all) = lax.scan(one_slab, start, jnp.arange(N_EXPERT, dtype=jnp.int32))
    return (layer_sum.astype(jnp.bfloat16), grad_sum.astype(jnp.bfloat16), jnp.take(gate_all, partner, axis=0), jnp.take(up_all, partner, axis=0), jnp.take(down_all, partner, axis=0))
```

```python
import functools

import jax
import jax.numpy as jnp
from jax import lax
from jax.experimental import pallas as pl
from jax.experimental.pallas import tpu as pltpu
from jax.sharding import Mesh, PartitionSpec as P

TOK = 64
CAP = 40
FEAT = 448
WIDE = 512
HID = 512
QUAD = 4 * TOK
QROWS = 4 * CAP
HALF = 2 * CAP
QUADS = 8
TAIL = 3
ROWS = QUADS * QROWS
BUNDLE = 256
BF = jnp.bfloat16
F32 = jnp.float32


def dot(lhs, rhs):
    return jnp.dot(lhs, rhs, preferred_element_type=F32)


def dot_last(lhs, rhs):
    return lax.dot_general(lhs, rhs, (((1,), (1,)), ((), ())), preferred_element_type=F32)


def dot_first(lhs, rhs):
    return lax.dot_general(lhs, rhs, (((0,), (0,)), ((), ())), preferred_element_type=F32)


def weight_rows(tail, experts):
    lane = lax.broadcasted_iota(jnp.int32, (8, 128), 1)
    row = lax.broadcasted_iota(jnp.int32, (8, 128), 0)
    hit = lane < 0
    for i, expert in enumerate(experts):
        hit = hit | ((row == i) & (lane == TOK + expert))
    return dot_last(jnp.where(hit, 1.0, 0.0).astype(BF), tail)


def slot_places(weights):
    count = weights.shape[1]
    routed = weights > 0.0
    source = lax.broadcasted_iota(jnp.int32, (count, count), 0)
    target = lax.broadcasted_iota(jnp.int32, (count, count), 1)
    earlier = (source < target) & ((source >> 6) == (target >> 6))
    position = dot(jnp.where(routed, 1.0, 0.0).astype(BF), jnp.where(earlier, 1.0, 0.0).astype(BF))
    group = lax.broadcasted_iota(jnp.int32, weights.shape, 1) >> 6
    return jnp.where(routed, position.astype(jnp.int32) + CAP * group, -1)


def one_hot(place, rows):
    return lax.broadcasted_iota(jnp.int32, (rows, place.shape[1]), 0) == place


def quad_select(tail, expert):
    weights = weight_rows(tail, (expert,))
    place = slot_places(weights)
    return weights[0:1], place[0:1]


def slot_weights(hit, weights):
    return jnp.sum(jnp.where(hit, weights, 0.0), axis=1, keepdims=True)


def as_matrix(hit):
    return jnp.where(hit, 1.0, 0.0).astype(BF)


def own_half_first(place, core):
    moved = place - HALF * core
    return jnp.where(place < 0, -1, jnp.where(moved < 0, moved + QROWS, moved))


def gate_up_kernel(info, tok_ref, gate_ref, up_ref, keep_ref, send_ref):
    weights, place = quad_select(tok_ref[:, TAIL * 128 :], info[0])
    pick = as_matrix(one_hot(own_half_first(place, info[1]), QROWS))
    rows = dot(pick, tok_ref[:, :FEAT]).astype(BF)
    gate = dot(rows, gate_ref[...]).astype(BF)
    up = dot(rows, up_ref[...]).astype(BF)
    keep_ref[0, :, :HID] = gate[:HALF]
    keep_ref[0, :, HID:] = up[:HALF]
    send_ref[0, :, :HID] = gate[HALF:]
    send_ref[0, :, HID:] = up[HALF:]


def hidden_grad_kernel(info, tail_ref, cot_ref, down_ref, keep_ref, send_ref):
    weights, place = quad_select(tail_ref[...], info[0])
    hit = one_hot(own_half_first(place, info[1]), QROWS)
    scaled = (slot_weights(hit, weights) * dot(as_matrix(hit), cot_ref[:, :FEAT])).astype(BF)
    grad = dot_last(scaled, down_ref[...]).astype(BF)
    keep_ref[0] = grad[:HALF]
    send_ref[0] = grad[HALF:]


def activation_kernel(gate_up_ref, grad_ref, out_ref):
    both = jnp.sum(gate_up_ref[...].astype(F32), axis=0)
    gate, up = both[:, :HID], both[:, HID:]
    grad = jnp.sum(grad_ref[...].astype(F32), axis=0)
    sig = jax.nn.sigmoid(gate)
    activated = gate * sig
    out_ref[0:HALF] = (activated * up).astype(BF)
    out_ref[HALF : 2 * HALF] = (grad * up * sig * (1.0 + gate * (1.0 - sig))).astype(BF)
    out_ref[2 * HALF : 3 * HALF] = (grad * activated).astype(BF)
    out_ref[3 * HALF :] = jnp.zeros((BUNDLE - 3 * HALF, HID), BF)


def bundle_part(acts_ref, part):
    picked = acts_ref[:, part * HALF : (part + 1) * HALF, :]
    return picked.reshape(picked.shape[0] * HALF, HID)


def terms_kernel(info, tail_ref, acts_ref, gate_ref, up_ref, down_ref, out_ref):
    weights, place = quad_select(tail_ref[...], info[0])
    factor = slot_weights(one_hot(place, QROWS), weights)
    out = (dot(bundle_part(acts_ref, 0), down_ref[...]) * factor).astype(BF)
    back = dot_last(bundle_part(acts_ref, 1), gate_ref[...]) + dot_last(bundle_part(acts_ref, 2), up_ref[...])
    out_ref[...] = jnp.concatenate([out, back.astype(BF)], axis=1)


def merge_kernel(info, tail_ref, rows_ref, out_ref):
    weights = weight_rows(tail_ref[...], tuple(info[4 + i] for i in range(4)))
    place = slot_places(weights)
    total = jnp.zeros(out_ref.shape, F32)
    for i in range(4):
        total = total + dot_first(as_matrix(one_hot(place[i : i + 1], HALF)), rows_ref[i])
    out_ref[...] = total.astype(BF)


def new_rows_kernel(info, tok_ref, cot_ref, rows_ref, scaled_ref):
    weights, place = quad_select(tok_ref[:, TAIL * 128 :], info[2])
    hit = one_hot(place, QROWS)
    pick = as_matrix(hit)
    rows_ref[...] = dot(pick, tok_ref[:, :FEAT]).astype(BF)
    scaled_ref[...] = (slot_weights(hit, weights) * dot(pick, cot_ref[:, :FEAT])).astype(BF)


def slab_grad_kernel(rows_ref, scaled_ref, acts_ref, gate_ref, up_ref, down_ref):
    gate_ref[...] = dot_first(rows_ref[...], bundle_part(acts_ref, 1)).astype(BF)
    up_ref[...] = dot_first(rows_ref[...], bundle_part(acts_ref, 2)).astype(BF)
    down_ref[...] = dot_first(bundle_part(acts_ref, 0), scaled_ref[...]).astype(BF)


def call(kernel, grid, in_specs, out_specs, out_shape, flops, moved, info, *operands):
    return pl.pallas_call(
        kernel,
        grid_spec=pltpu.PrefetchScalarGridSpec(
            num_scalar_prefetch=1, grid=grid, in_specs=in_specs, out_specs=out_specs
        ),
        out_shape=out_shape,
        compiler_params=pltpu.CompilerParams(vmem_limit_bytes=32 * 1024 * 1024),
        cost_estimate=pl.CostEstimate(flops=flops, bytes_accessed=moved, transcendentals=0),
    )(info, *operands)


def whole(*shape):
    return pl.BlockSpec(shape, lambda q, info: (0,) * len(shape))


def quad_block(*shape):
    return pl.BlockSpec(shape, lambda q, info: (q,) + (0,) * (len(shape) - 1))


def tail_block():
    return pl.BlockSpec((QUAD, 128), lambda q, info: (q, TAIL))


def shaped(*shape):
    return jax.ShapeDtypeStruct(shape, BF)


def swap(value):
    return lax.ppermute(value, "core", [(0, 1), (1, 0)])


def exchange(value, axes):
    return lax.all_to_all(value, axes, split_axis=0, concat_axis=0, tiled=True)


def dp_scatter_sum(keep, send):
    pair = (keep.astype(F32) + swap(send).astype(F32)).astype(BF)
    return exchange(pair, "z")


def body(tokens, cotangent, expert_ids, route_probs, held_before, partner, gate_slabs, up_slabs, down_slabs):
    gate, up, down = gate_slabs[0], up_slabs[0], down_slabs[0]
    here_y, here_x, core = lax.axis_index("y"), lax.axis_index("x"), lax.axis_index("core")
    here = here_y * 4 + here_x
    experts = held_before // 2
    new_expert = experts[partner[here]]
    row_experts = lax.dynamic_slice(experts, (here_y * 4,), (4,))
    info = jnp.concatenate(
        [jnp.stack([experts[here], core, new_expert, here_x]).astype(jnp.int32), row_experts.astype(jnp.int32)]
    )

    cot_all = lax.all_gather(jnp.pad(cotangent, ((0, 0), (0, WIDE - FEAT))), ("y", "x"), tiled=True)
    names = lax.broadcasted_iota(jnp.int32, (1, 1, 16), 2)
    dense = jnp.sum(
        jnp.where(expert_ids[:, :, None] == names, route_probs[:, :, None].astype(F32), 0.0), axis=1
    ).astype(BF)
    packed = jnp.concatenate([tokens, dense, jnp.zeros((TOK, WIDE - FEAT - 16), BF)], axis=1)
    column = exchange(jnp.broadcast_to(packed, (8, TOK, WIDE)), "y").reshape(8 * TOK, WIDE)
    tok_all = exchange(jnp.broadcast_to(column, (4, 8 * TOK, WIDE)), "x").reshape(32 * TOK, WIDE)

    halves = (quad_block(1, HALF, 2 * HID), quad_block(1, HALF, 2 * HID))
    keep, send = call(
        gate_up_kernel,
        (QUADS,),
        [quad_block(QUAD, WIDE), whole(FEAT, HID), whole(FEAT, HID)],
        halves,
        (shaped(QUADS, HALF, 2 * HID), shaped(QUADS, HALF, 2 * HID)),
        3_000_000_000,
        6_000_000,
        info,
        tok_all,
        gate,
        up,
    )
    gate_up = dp_scatter_sum(keep, send)

    cot_spec = pl.BlockSpec((4, 1, TOK, WIDE), lambda q, info: (q % 2, q // 2, 0, 0))
    cot_view = cot_all.reshape(2, 4, 4, TOK, WIDE)
    cot_spec = pl.BlockSpec((None, 4, None, TOK, WIDE), lambda q, info: (q % 2, 0, q // 2, 0, 0))

    def with_cot(kernel, position):
        def run(*refs):
            refs = list(refs)
            refs[position] = _Flat(refs[position])
            kernel(*refs)

        return run

    keep, send = call(
        with_cot(hidden_grad_kernel, 2),
        (QUADS,),
        [tail_block(), cot_spec, whole(HID, FEAT)],
        (quad_block(1, HALF, HID), quad_block(1, HALF, HID)),
        (shaped(QUADS, HALF, HID), shaped(QUADS, HALF, HID)),
        1_500_000_000,
        5_000_000,
        info,
        tok_all,
        cot_view,
        down,
    )
    hidden_grad = dp_scatter_sum(keep, send)

    acts = pl.pallas_call(
        activation_kernel,
        out_shape=shaped(BUNDLE, HID),
        compiler_params=pltpu.CompilerParams(vmem_limit_bytes=32 * 1024 * 1024),
        cost_estimate=pl.CostEstimate(flops=3_000_000, bytes_accessed=2_300_000, transcendentals=50_000),
    )(gate_up, hidden_grad)

    own_acts = lax.all_gather(acts, ("z", "core"), tiled=True).reshape(16, BUNDLE, HID)
    spread = exchange(acts.reshape(32, 8, HID), ("y", "x"))
    moved = exchange(jnp.take(spread, partner, axis=0), ("y", "x")).reshape(BUNDLE, HID)

    terms = call(
        terms_kernel,
        (QUADS,),
        [tail_block(), quad_block(2, BUNDLE, HID), whole(FEAT, HID), whole(FEAT, HID), whole(HID, FEAT)],
        quad_block(QROWS, 2 * FEAT),
        shaped(ROWS, 2 * FEAT),
        2_000_000_000,
        8_000_000,
        info,
        tok_all,
        own_acts,
        gate,
        up,
        down,
    )
    new_acts = lax.all_gather(moved, ("z", "core"), tiled=True).reshape(16, BUNDLE, HID)

    returned = exchange(terms.reshape(4, 8 * CAP, 2 * FEAT), "x")
    merged = call(
        merge_kernel,
        (4,),
        [
            pl.BlockSpec((2 * TOK, 128), lambda q, info: (info[3] * 4 + q, TAIL)),
            pl.BlockSpec((4, HALF, 2 * FEAT), lambda q, info: (0, q, 0)),
        ],
        quad_block(2 * TOK, 2 * FEAT),
        shaped(8 * TOK, 2 * FEAT),
        300_000_000,
        3_500_000,
        info,
        tok_all,
        returned,
    )
    home = exchange(merged.reshape(8, TOK, 2 * FEAT), "y")

    rows, scaled = call(
        with_cot(new_rows_kernel, 2),
        (QUADS,),
        [quad_block(QUAD, WIDE), cot_spec],
        (quad_block(QROWS, FEAT), quad_block(QROWS, FEAT)),
        (shaped(ROWS, FEAT), shaped(ROWS, FEAT)),
        600_000_000,
        6_500_000,
        info,
        tok_all,
        cot_view,
    )
    gate_grad, up_grad, down_grad = pl.pallas_call(
        slab_grad_kernel,
        out_shape=(shaped(FEAT, HID), shaped(FEAT, HID), shaped(HID, FEAT)),
        compiler_params=pltpu.CompilerParams(vmem_limit_bytes=32 * 1024 * 1024),
        cost_estimate=pl.CostEstimate(flops=1_800_000_000, bytes_accessed=8_000_000, transcendentals=0),
    )(rows, scaled, new_acts)

    total = jnp.sum(home.astype(F32), axis=0).astype(BF)
    return (total[:, :FEAT], total[:, FEAT:], gate_grad[None], up_grad[None], down_grad[None])


class _Flat:
    def __init__(self, ref):
        self.ref = ref

    def __getitem__(self, index):
        return self.ref[...].reshape(QUAD, WIDE)[index]


def solution(mesh):
    fine = Mesh(mesh.devices.reshape(8, 4, 8, 2), ("y", "x", "z", "core"))
    expert, dp = ("y", "x"), ("z", "core")
    return jax.shard_map(
        body,
        mesh=fine,
        in_specs=(
            P(expert, dp),
            P(expert, dp),
            P(expert, None),
            P(expert, None),
            P(),
            P(),
            P(expert, dp, None),
            P(expert, dp, None),
            P(expert, None, dp),
        ),
        out_specs=(
            P(expert, dp),
            P(expert, dp),
            P(expert, dp, None),
            P(expert, dp, None),
            P(expert, None, dp),
        ),
        check_vma=False,
    )
```

```python
import jax
import jax.numpy as jnp
from jax import lax
from jax.experimental import pallas as pl
from jax.experimental.pallas import tpu as pltpu
from jax.sharding import Mesh, PartitionSpec as P

TOK = 64
CAP = 40
FEAT = 448
WIDE = 512
HID = 512
PAIR = 2 * TOK
HALF = 2 * CAP
CHUNKS = 16
ROWS = CHUNKS * HALF
BUNDLE = 256
BF = jnp.bfloat16
F32 = jnp.float32


def dot(lhs, rhs):
    return jnp.dot(lhs, rhs, preferred_element_type=F32)


def dot_last(lhs, rhs):
    return lax.dot_general(lhs, rhs, (((1,), (1,)), ((), ())), preferred_element_type=F32)


def dot_first(lhs, rhs):
    return lax.dot_general(lhs, rhs, (((0,), (0,)), ((), ())), preferred_element_type=F32)


def as_matrix(hit):
    return jnp.where(hit, 1.0, 0.0).astype(BF)


def weight_rows(tail, experts):
    lane = lax.broadcasted_iota(jnp.int32, (8, 128), 1)
    row = lax.broadcasted_iota(jnp.int32, (8, 128), 0)
    hit = lane < 0
    for i, expert in enumerate(experts):
        hit = hit | ((row == i) & (lane == TOK + expert))
    return dot_last(as_matrix(hit), tail)


def slot_places(weights):
    count = weights.shape[1]
    routed = weights > 0.0
    source = lax.broadcasted_iota(jnp.int32, (count, count), 0)
    target = lax.broadcasted_iota(jnp.int32, (count, count), 1)
    earlier = (source < target) & ((source >> 6) == (target >> 6))
    position = dot(as_matrix(routed), as_matrix(earlier))
    group = lax.broadcasted_iota(jnp.int32, weights.shape, 1) >> 6
    return jnp.where(routed, position.astype(jnp.int32) + CAP * group, -1)


def one_hot(place, rows):
    return lax.broadcasted_iota(jnp.int32, (rows, place.shape[1]), 0) == place


def chunk_hits(tail, expert):
    weights = weight_rows(tail, (expert,))
    return one_hot(slot_places(weights)[0:1], HALF), weights[0:1]


def slot_weights(hit, weights):
    return jnp.sum(jnp.where(hit, weights, 0.0), axis=1, keepdims=True)


def prep_kernel(tok_ref, cot_ref, ids_ref, probs_ref, held_ref, packed_ref, sent_ref):
    names = lax.broadcasted_iota(jnp.int32, (TOK, TOK), 1)
    probs = probs_ref[...].astype(F32)
    ids = ids_ref[...]
    dense = jnp.zeros((TOK, TOK), F32)
    for k in range(8):
        dense = dense + jnp.where(ids[:, k : k + 1] == names, probs[:, k : k + 1], 0.0)
    dense = dense.astype(BF)
    tok = jnp.concatenate([tok_ref[...], dense], axis=1)
    packed_ref[:, :WIDE] = jnp.concatenate([cot_ref[...], dense], axis=1)
    packed_ref[:, WIDE:] = tok
    slab = lax.broadcasted_iota(jnp.int32, (32, TOK), 1) == (held_ref[...] >> 1)
    place = slot_places(dot_last(as_matrix(slab), dense))
    first = lax.broadcasted_iota(jnp.int32, (HALF, TOK), 0) < CAP
    slot = lax.broadcasted_iota(jnp.int32, (HALF, TOK), 0)
    slot = jnp.where(first, slot, slot - CAP)
    for i in range(CHUNKS):
        hit = slot == jnp.where(first, place[2 * i : 2 * i + 1], place[2 * i + 1 : 2 * i + 2])
        sent_ref[i] = dot(as_matrix(hit), tok).astype(BF)


def gate_up(rows_ref, gate_ref, up_ref):
    count = rows_ref.shape[0] * HALF
    rows = rows_ref[...].reshape(count, WIDE)[:, :FEAT]
    return dot(rows, gate_ref[...]), dot(rows, up_ref[...])


def gate_up_send_kernel(info, rows_ref, gate_ref, up_ref, out_ref):
    gate, up = gate_up(rows_ref, gate_ref, up_ref)
    shape = (rows_ref.shape[0], HALF, HID)
    out_ref[:, :, :HID] = gate.astype(BF).reshape(shape)
    out_ref[:, :, HID:] = up.astype(BF).reshape(shape)


def gate_up_keep_kernel(info, rows_ref, gate_ref, up_ref, got_ref, out_ref):
    gate, up = gate_up(rows_ref, gate_ref, up_ref)
    shape = (rows_ref.shape[0], HALF, HID)
    out_ref[:, :, :HID] = (gate.reshape(shape) + got_ref[:, :, :HID].astype(F32)).astype(BF)
    out_ref[:, :, HID:] = (up.reshape(shape) + got_ref[:, :, HID:].astype(F32)).astype(BF)


def hidden_grad(info, cot_ref, down_ref):
    parts = []
    for i in range(cot_ref.shape[0]):
        hit, weights = chunk_hits(cot_ref[i, :, WIDE - 128 :], info[0])
        rows = dot(as_matrix(hit), cot_ref[i, :, :FEAT])
        parts.append((slot_weights(hit, weights) * rows).astype(BF))
    grad = dot_last(jnp.concatenate(parts, axis=0), down_ref[...])
    return grad.reshape(cot_ref.shape[0], HALF, HID)


def hidden_grad_send_kernel(info, cot_ref, down_ref, after_ref, out_ref):
    out_ref[...] = hidden_grad(info, cot_ref, down_ref).astype(BF)


def hidden_grad_keep_kernel(info, cot_ref, down_ref, got_ref, after_ref, out_ref):
    out_ref[...] = (hidden_grad(info, cot_ref, down_ref) + got_ref[...].astype(F32)).astype(BF)


def activation_kernel(gate_up_ref, grad_ref, out_ref):
    both = jnp.sum(gate_up_ref[...].astype(F32), axis=0)
    gate, up = both[:, :HID], both[:, HID:]
    grad = jnp.sum(grad_ref[...].astype(F32), axis=0)
    sig = jax.nn.sigmoid(gate)
    activated = gate * sig
    out_ref[0:HALF] = (activated * up).astype(BF)
    out_ref[HALF : 2 * HALF] = (grad * up * sig * (1.0 + gate * (1.0 - sig))).astype(BF)
    out_ref[2 * HALF : 3 * HALF] = (grad * activated).astype(BF)
    out_ref[3 * HALF :] = jnp.zeros((BUNDLE - 3 * HALF, HID), BF)


def pick_kernel(partner, pieces_ref, out_ref):
    for j in range(32):
        out_ref[j] = pieces_ref[partner[j]]


def bundle_part(acts_ref, part):
    picked = acts_ref[:, part * HALF : (part + 1) * HALF, :]
    return picked.reshape(picked.shape[0] * HALF, HID)


def terms_kernel(info, tail_ref, acts_ref, gate_ref, up_ref, down_ref, out_ref):
    lane = lax.broadcasted_iota(jnp.int32, tail_ref.shape, 1)
    factor = jnp.sum(jnp.where(lane == TOK + info[0], tail_ref[...].astype(F32), 0.0), axis=1, keepdims=True)
    out = dot(bundle_part(acts_ref, 0), down_ref[...]) * factor
    back = dot_last(bundle_part(acts_ref, 1), gate_ref[...]) + dot_last(bundle_part(acts_ref, 2), up_ref[...])
    both = jnp.concatenate([out, back], axis=1)
    for y in range(out_ref.shape[1]):
        for x in range(4):
            at = (4 * y + x) * CAP
            out_ref[x, y] = both[at : at + CAP].astype(BF)


def merge_kernel(info, tail_ref, rows_ref, out_ref):
    weights = weight_rows(tail_ref[...].reshape(PAIR, 128), tuple(info[4 + i] for i in range(4)))
    place = slot_places(weights)
    total = jnp.zeros(out_ref.shape, F32)
    for i in range(4):
        total = total + dot_first(as_matrix(one_hot(place[i : i + 1], HALF)), rows_ref[i])
    out_ref[...] = total.astype(BF)


def new_rows_kernel(info, packed_ref, rows_ref, scaled_ref):
    for i in range(packed_ref.shape[0]):
        hit, weights = chunk_hits(packed_ref[i, :, WIDE - 128 : WIDE], info[2])
        pick = as_matrix(hit)
        rows_ref[i] = dot(pick, packed_ref[i, :, WIDE : WIDE + FEAT]).astype(BF)
        scaled_ref[i] = (slot_weights(hit, weights) * dot(pick, packed_ref[i, :, :FEAT])).astype(BF)


def slab_grad_kernel(rows_ref, scaled_ref, acts_ref, gate_ref, up_ref, down_ref):
    gate_ref[...] = dot_first(rows_ref[...], bundle_part(acts_ref, 1)).astype(BF)
    up_ref[...] = dot_first(rows_ref[...], bundle_part(acts_ref, 2)).astype(BF)
    down_ref[...] = dot_first(bundle_part(acts_ref, 0), scaled_ref[...]).astype(BF)


def shaped(*shape):
    return jax.ShapeDtypeStruct(shape, BF)


def params():
    return pltpu.CompilerParams(vmem_limit_bytes=32 * 1024 * 1024)


def cost(mflop, kbytes):
    return pl.CostEstimate(flops=mflop * 1_000_000, bytes_accessed=kbytes * 1000, transcendentals=0)


def call(kernel, grid, in_specs, out_specs, out_shape, estimate, info, *operands):
    return pl.pallas_call(
        kernel,
        grid_spec=pltpu.PrefetchScalarGridSpec(
            num_scalar_prefetch=1, grid=grid, in_specs=in_specs, out_specs=out_specs
        ),
        out_shape=out_shape,
        compiler_params=params(),
        cost_estimate=estimate,
    )(info, *operands)


def local(kernel, out_shape, estimate, *operands):
    return pl.pallas_call(kernel, out_shape=out_shape, compiler_params=params(), cost_estimate=estimate)(*operands)


def whole(*shape):
    return pl.BlockSpec(shape, lambda i, info: (0,) * len(shape))


def lead_block(*shape):
    return pl.BlockSpec(shape, lambda i, info: (i,) + (0,) * (len(shape) - 1))


def core_half(count, rows, lanes, mine):
    if mine:
        return pl.BlockSpec((count, None, rows, lanes), lambda i, info: (i, info[1], 0, 0))
    return pl.BlockSpec((count, None, rows, lanes), lambda i, info: (i, 1 - info[1], 0, 0))


ANYWHERE = pl.BlockSpec(memory_space=pl.ANY)


def swap(value):
    return lax.ppermute(value, "core", [(0, 1), (1, 0)])


def exchange(value, axes):
    return lax.all_to_all(value, axes, split_axis=0, concat_axis=0, tiled=True)


def body(tokens, cotangent, expert_ids, route_probs, held_before, partner, gate_slabs, up_slabs, down_slabs):
    gate, up, down = gate_slabs[0], up_slabs[0], down_slabs[0]
    here_y, here_x, core = lax.axis_index("y"), lax.axis_index("x"), lax.axis_index("core")
    here = here_y * 4 + here_x
    experts = held_before // 2
    new_expert = experts[partner[here]]
    row_experts = lax.dynamic_slice(experts, (here_y * 4,), (4,))
    info = jnp.concatenate(
        [jnp.stack([experts[here], core, new_expert, here_x]).astype(jnp.int32), row_experts.astype(jnp.int32)]
    )

    packed, sent = local(
        prep_kernel,
        (shaped(TOK, 2 * WIDE), shaped(CHUNKS, HALF, WIDE)),
        cost(90, 1600),
        tokens,
        cotangent,
        expert_ids,
        route_probs,
        held_before.reshape(32, 1),
    )
    everyone = lax.all_gather(packed, ("y", "x"), tiled=True)
    own_rows = exchange(sent.reshape(32, CAP, WIDE), ("y", "x"))

    rows_view = own_rows.reshape(8, 2, HALF, WIDE)
    weight_specs = [whole(FEAT, HID), whole(FEAT, HID)]
    wide_out = lead_block(4, HALF, 2 * HID)
    sending = call(
        gate_up_send_kernel,
        (2,),
        [core_half(4, HALF, WIDE, False)] + weight_specs,
        wide_out,
        shaped(8, HALF, 2 * HID),
        cost(600, 2900),
        info,
        rows_view,
        gate,
        up,
    )
    pair_gate_up = call(
        gate_up_keep_kernel,
        (2,),
        [core_half(4, HALF, WIDE, True)] + weight_specs + [wide_out],
        wide_out,
        shaped(8, HALF, 2 * HID),
        cost(600, 4200),
        info,
        rows_view,
        gate,
        up,
        swap(sending),
    )
    sums_gate_up = exchange(pair_gate_up, "z")

    cot_view = everyone.reshape(8, 2, PAIR, 2 * WIDE)
    thin_out = lead_block(4, HALF, HID)
    sending = call(
        hidden_grad_send_kernel,
        (2,),
        [core_half(4, PAIR, WIDE, False), whole(HID, FEAT), ANYWHERE],
        thin_out,
        shaped(8, HALF, HID),
        cost(400, 2200),
        info,
        cot_view,
        down,
        pair_gate_up,
    )
    pair_grad = call(
        hidden_grad_keep_kernel,
        (2,),
        [core_half(4, PAIR, WIDE, True), whole(HID, FEAT), thin_out, ANYWHERE],
        thin_out,
        shaped(8, HALF, HID),
        cost(400, 2900),
        info,
        cot_view,
        down,
        swap(sending),
        sums_gate_up,
    )
    sums_grad = exchange(pair_grad, "z")

    acts = local(activation_kernel, shaped(BUNDLE, HID), cost(3, 2300), sums_gate_up, sums_grad)

    own_acts = lax.all_gather(acts, ("z", "core"), tiled=True).reshape(CHUNKS, BUNDLE, HID)
    pieces = exchange(acts.reshape(32, 8, HID), ("y", "x"))
    picked = pl.pallas_call(
        pick_kernel,
        grid_spec=pltpu.PrefetchScalarGridSpec(
            num_scalar_prefetch=1,
            grid=(1,),
            in_specs=[whole(32, 8, HID)],
            out_specs=whole(32, 8, HID),
        ),
        out_shape=shaped(32, 8, HID),
        compiler_params=params(),
        cost_estimate=cost(1, 520),
    )(partner, pieces)
    moved = exchange(picked, ("y", "x")).reshape(BUNDLE, HID)

    terms = call(
        terms_kernel,
        (4,),
        [
            pl.BlockSpec((4 * HALF, 128), lambda i, info: (i, 3)),
            lead_block(4, BUNDLE, HID),
            whole(FEAT, HID),
            whole(FEAT, HID),
            whole(HID, FEAT),
        ],
        pl.BlockSpec((4, 2, CAP, 2 * FEAT), lambda i, info: (0, i, 0, 0)),
        shaped(4, 8, CAP, 2 * FEAT),
        cost(1800, 8000),
        info,
        own_rows.reshape(ROWS, WIDE),
        own_acts,
        gate,
        up,
        down,
    )
    new_acts = lax.all_gather(moved, ("z", "core"), tiled=True).reshape(CHUNKS, BUNDLE, HID)

    returned = exchange(terms.reshape(4, 8 * CAP, 2 * FEAT), "x")
    merged = call(
        merge_kernel,
        (4,),
        [
            pl.BlockSpec((2, None, TOK, 128), lambda i, info: (i, info[3], 0, 3)),
            pl.BlockSpec((4, HALF, 2 * FEAT), lambda i, info: (0, i, 0)),
        ],
        lead_block(PAIR, 2 * FEAT),
        shaped(8 * TOK, 2 * FEAT),
        cost(300, 3500),
        info,
        everyone.reshape(8, 4, TOK, 2 * WIDE),
        returned,
    )
    home = exchange(merged.reshape(8, TOK, 2 * FEAT), "y")

    rows, scaled = call(
        new_rows_kernel,
        (4,),
        [lead_block(4, PAIR, 2 * WIDE)],
        (lead_block(4, HALF, FEAT), lead_block(4, HALF, FEAT)),
        (shaped(CHUNKS, HALF, FEAT), shaped(CHUNKS, HALF, FEAT)),
        cost(600, 6500),
        info,
        everyone.reshape(CHUNKS, PAIR, 2 * WIDE),
    )
    gate_grad, up_grad, down_grad = local(
        slab_grad_kernel,
        (shaped(FEAT, HID), shaped(FEAT, HID), shaped(HID, FEAT)),
        cost(1800, 8000),
        rows.reshape(ROWS, FEAT),
        scaled.reshape(ROWS, FEAT),
        new_acts,
    )

    total = jnp.sum(home.astype(F32), axis=0).astype(BF)
    return (total[:, :FEAT], total[:, FEAT:], gate_grad[None], up_grad[None], down_grad[None])


def solution(mesh):
    fine = Mesh(mesh.devices.reshape(8, 4, 8, 2), ("y", "x", "z", "core"))
    expert, dp = ("y", "x"), ("z", "core")
    slab = P(expert, dp, None)
    down = P(expert, None, dp)
    return jax.shard_map(
        body,
        mesh=fine,
        in_specs=(P(expert, dp), P(expert, dp), P(expert, None), P(expert, None), P(), P(), slab, slab, down),
        out_specs=(P(expert, dp), P(expert, dp), slab, slab, down),
        check_vma=False,
    )
```

```python
import jax
import jax.numpy as jnp
from jax import lax
from jax.experimental import pallas as pl
from jax.experimental.pallas import tpu as pltpu
from jax.sharding import Mesh, PartitionSpec as P

TOK = 64
CAP = 40
FEAT = 448
WIDE = 512
HID = 512
PAIR = 2 * TOK
HALF = 2 * CAP
CHUNKS = 16
ROWS = CHUNKS * HALF
BUNDLE = 256
BF = jnp.bfloat16
F32 = jnp.float32


def dot(lhs, rhs):
    return jnp.dot(lhs, rhs, preferred_element_type=F32)


def dot_last(lhs, rhs):
    return lax.dot_general(lhs, rhs, (((1,), (1,)), ((), ())), preferred_element_type=F32)


def dot_first(lhs, rhs):
    return lax.dot_general(lhs, rhs, (((0,), (0,)), ((), ())), preferred_element_type=F32)


def as_matrix(hit):
    return jnp.where(hit, 1.0, 0.0).astype(BF)


def weight_rows(tail, experts):
    lane = lax.broadcasted_iota(jnp.int32, (8, 128), 1)
    row = lax.broadcasted_iota(jnp.int32, (8, 128), 0)
    hit = lane < 0
    for i, expert in enumerate(experts):
        hit = hit | ((row == i) & (lane == TOK + expert))
    return dot_last(as_matrix(hit), tail)


def slot_places(weights):
    count = weights.shape[1]
    routed = weights > 0.0
    source = lax.broadcasted_iota(jnp.int32, (count, count), 0)
    target = lax.broadcasted_iota(jnp.int32, (count, count), 1)
    earlier = (source < target) & ((source >> 6) == (target >> 6))
    position = dot(as_matrix(routed), as_matrix(earlier))
    group = lax.broadcasted_iota(jnp.int32, weights.shape, 1) >> 6
    return jnp.where(routed, position.astype(jnp.int32) + CAP * group, -1)


def one_hot(place, rows):
    return lax.broadcasted_iota(jnp.int32, (rows, place.shape[1]), 0) == place


def chunk_hits(tail, expert):
    weights = weight_rows(tail, (expert,))
    return one_hot(slot_places(weights)[0:1], HALF), weights[0:1]


def slot_weights(hit, weights):
    return jnp.sum(jnp.where(hit, weights, 0.0), axis=1, keepdims=True)


def prep_kernel(held, tok_ref, cot_ref, ids_ref, probs_ref, packed_ref, sent_ref):
    def weights_of(names):
        return sum(jnp.where(ids_ref[k : k + 1] == names, probs_ref[k : k + 1].astype(F32), 0.0) for k in range(8))

    names = lax.broadcasted_iota(jnp.int32, (TOK, TOK), 0)
    same = names == lax.broadcasted_iota(jnp.int32, (TOK, TOK), 1)
    dense = dot_first(weights_of(names).astype(BF), as_matrix(same)).astype(BF)
    tok, cot = tok_ref[...], cot_ref[...]
    packed_ref[:, :WIDE] = jnp.concatenate([cot, dense], axis=1)
    packed_ref[:, WIDE:] = jnp.concatenate([tok, dense], axis=1)

    slab = lax.broadcasted_iota(jnp.int32, (32, TOK), 0)
    expert = jnp.zeros((32, TOK), jnp.int32)
    for i in range(32):
        expert = jnp.where(slab == i, held[i] >> 1, expert)
    weights = weights_of(expert)
    place = slot_places(weights)
    first = lax.broadcasted_iota(jnp.int32, (HALF, TOK), 0) < CAP
    slot = lax.broadcasted_iota(jnp.int32, (HALF, TOK), 0)
    slot = jnp.where(first, slot, slot - CAP)
    for i in range(CHUNKS):
        one, two = slice(2 * i, 2 * i + 1), slice(2 * i + 1, 2 * i + 2)
        hit = slot == jnp.where(first, place[one], place[two])
        factor = slot_weights(hit, jnp.where(first, weights[one], weights[two]))
        pick = as_matrix(hit)
        rows = dot(pick, tok)
        scaled = factor * dot(pick, cot)
        sent_ref[i] = jnp.concatenate([rows, scaled], axis=1).astype(BF)


def products(rows_ref, gate_ref, up_ref, down_ref):
    count = rows_ref.shape[0]
    rows = rows_ref[...].reshape(count * HALF, 2 * FEAT)
    tok, scaled = rows[:, :FEAT], rows[:, FEAT:]
    three = dot(tok, gate_ref[...]), dot(tok, up_ref[...]), dot(scaled, down_ref[...])
    return [(slice(i * HID, (i + 1) * HID), part.reshape(count, HALF, HID)) for i, part in enumerate(three)]


def send_kernel(coords, rows_ref, gate_ref, up_ref, down_ref, out_ref):
    for lanes, part in products(rows_ref, gate_ref, up_ref, down_ref):
        out_ref[:, :, lanes] = part.astype(BF)


def keep_kernel(coords, rows_ref, gate_ref, up_ref, down_ref, got_ref, out_ref):
    for lanes, part in products(rows_ref, gate_ref, up_ref, down_ref):
        out_ref[:, :, lanes] = (part + got_ref[:, :, lanes].astype(F32)).astype(BF)


def activation_kernel(sums_ref, out_ref):
    sums = jnp.sum(sums_ref[...].astype(F32), axis=0)
    gate, up, grad = sums[:, :HID], sums[:, HID : 2 * HID], sums[:, 2 * HID :]
    sig = jax.nn.sigmoid(gate)
    activated = gate * sig
    out_ref[0:HALF] = (activated * up).astype(BF)
    out_ref[HALF : 2 * HALF] = (grad * up * sig * (1.0 + gate * (1.0 - sig))).astype(BF)
    out_ref[2 * HALF : 3 * HALF] = (grad * activated).astype(BF)
    out_ref[3 * HALF :] = jnp.zeros((BUNDLE - 3 * HALF, HID), BF)


def pick_kernel(partner, pieces_ref, out_ref):
    for j in range(32):
        out_ref[j] = pieces_ref[partner[j]]


def bundle_part(acts_ref, part):
    picked = acts_ref[:, part * HALF : (part + 1) * HALF, :]
    return picked.reshape(picked.shape[0] * HALF, HID)


def terms_kernel(coords, acts_ref, gate_ref, up_ref, down_ref, out_ref):
    out = dot_last(bundle_part(acts_ref, 0), down_ref[...])
    back = dot_last(bundle_part(acts_ref, 1), gate_ref[...]) + dot_last(bundle_part(acts_ref, 2), up_ref[...])
    both = jnp.concatenate([out, back], axis=1)
    for y in range(out_ref.shape[1]):
        for x in range(4):
            at = (4 * y + x) * CAP
            out_ref[x, y] = both[at : at + CAP].astype(BF)


def merge_kernel(held, coords, tail_ref, rows_ref, out_ref):
    weights = weight_rows(tail_ref[...].reshape(PAIR, 128), tuple(held[4 * coords[0] + i] >> 1 for i in range(4)))
    place = slot_places(weights)
    out = jnp.zeros(out_ref.shape, F32)
    back = jnp.zeros(out_ref.shape, F32)
    for i in range(4):
        hit = one_hot(place[i : i + 1], HALF)
        out = out + dot_first(jnp.where(hit, weights[i : i + 1], 0.0).astype(BF), rows_ref[i])
        back = back + dot_first(as_matrix(hit), rows_ref[i])
    lane = lax.broadcasted_iota(jnp.int32, out_ref.shape, 1)
    out_ref[...] = jnp.where(lane < FEAT, out, back).astype(BF)


def new_rows_kernel(held, partner, coords, packed_ref, rows_ref, scaled_ref):
    expert = held[partner[4 * coords[0] + coords[1]]] >> 1
    for i in range(packed_ref.shape[0]):
        hit, weights = chunk_hits(packed_ref[i, :, WIDE - 128 : WIDE], expert)
        pick = as_matrix(hit)
        rows_ref[i] = dot(pick, packed_ref[i, :, WIDE : WIDE + FEAT]).astype(BF)
        scaled_ref[i] = (slot_weights(hit, weights) * dot(pick, packed_ref[i, :, :FEAT])).astype(BF)


def slab_grad_kernel(rows_ref, scaled_ref, acts_ref, gate_ref, up_ref, down_ref):
    gate_ref[...] = dot_first(rows_ref[...], bundle_part(acts_ref, 1)).astype(BF)
    up_ref[...] = dot_first(rows_ref[...], bundle_part(acts_ref, 2)).astype(BF)
    down_ref[...] = dot_first(scaled_ref[...], bundle_part(acts_ref, 0)).astype(BF)


def shaped(*shape):
    return jax.ShapeDtypeStruct(shape, BF)


def params():
    return pltpu.CompilerParams(vmem_limit_bytes=32 * 1024 * 1024)


def cost(mflop, kbytes):
    return pl.CostEstimate(flops=mflop * 1_000_000, bytes_accessed=kbytes * 1000, transcendentals=0)


def call(kernel, grid, in_specs, out_specs, out_shape, estimate, scalars, *operands):
    return pl.pallas_call(
        kernel,
        grid_spec=pltpu.PrefetchScalarGridSpec(
            num_scalar_prefetch=len(scalars), grid=grid, in_specs=in_specs, out_specs=out_specs
        ),
        out_shape=out_shape,
        compiler_params=params(),
        cost_estimate=estimate,
    )(*scalars, *operands)


def local(kernel, out_shape, estimate, *operands):
    return pl.pallas_call(kernel, out_shape=out_shape, compiler_params=params(), cost_estimate=estimate)(*operands)


def whole(*shape):
    return pl.BlockSpec(shape, lambda i, *scalars: (0,) * len(shape))


def lead_block(*shape):
    return pl.BlockSpec(shape, lambda i, *scalars: (i,) + (0,) * (len(shape) - 1))


def core_half(count, rows, lanes, mine):
    if mine:
        return pl.BlockSpec((count, None, rows, lanes), lambda i, coords: (i, coords[2], 0, 0))
    return pl.BlockSpec((count, None, rows, lanes), lambda i, coords: (i, 1 - coords[2], 0, 0))


def in_hbm(value):
    return pltpu.with_memory_space_constraint(value, pltpu.HBM)


def swap(value):
    return lax.ppermute(value, "core", [(0, 1), (1, 0)])


def exchange(value, axes):
    return lax.all_to_all(value, axes, split_axis=0, concat_axis=0, tiled=True)


def body(tokens, cotangent, expert_ids, route_probs, held_before, partner, gate_slabs, up_slabs, down_slabs):
    gate, up, down = gate_slabs[0], up_slabs[0], down_slabs[0].T
    coords = jnp.stack([lax.axis_index("y"), lax.axis_index("x"), lax.axis_index("core")]).astype(jnp.int32)

    packed, sent = call(
        prep_kernel,
        (1,),
        [whole(TOK, FEAT), whole(TOK, FEAT), whole(8, TOK), whole(8, TOK)],
        (whole(TOK, 2 * WIDE), whole(CHUNKS, HALF, 2 * FEAT)),
        (shaped(TOK, 2 * WIDE), shaped(CHUNKS, HALF, 2 * FEAT)),
        cost(150, 2600),
        (held_before,),
        tokens,
        cotangent,
        expert_ids.T,
        route_probs.T,
    )
    everyone = lax.all_gather(packed, ("y", "x"), tiled=True)
    own_rows = exchange(sent.reshape(32, CAP, 2 * FEAT), ("y", "x"))

    rows_view = own_rows.reshape(8, 2, HALF, 2 * FEAT)
    weight_specs = [whole(FEAT, HID), whole(FEAT, HID), whole(FEAT, HID)]
    sums_block = lead_block(4, HALF, 3 * HID)
    sending = call(
        send_kernel,
        (2,),
        [core_half(4, HALF, 2 * FEAT, False)] + weight_specs,
        sums_block,
        shaped(8, HALF, 3 * HID),
        cost(900, 4500),
        (coords,),
        rows_view,
        gate,
        up,
        down,
    )
    pairs = call(
        keep_kernel,
        (2,),
        [core_half(4, HALF, 2 * FEAT, True)] + weight_specs + [sums_block],
        sums_block,
        shaped(8, HALF, 3 * HID),
        cost(900, 6500),
        (coords,),
        rows_view,
        gate,
        up,
        down,
        swap(sending),
    )
    acts = local(activation_kernel, shaped(BUNDLE, HID), cost(3, 2300), exchange(pairs, "z"))

    own_acts = lax.all_gather(acts, ("z", "core"), tiled=True).reshape(CHUNKS, BUNDLE, HID)
    pieces = exchange(acts.reshape(32, 8, HID), ("y", "x"))
    picked = call(
        pick_kernel,
        (1,),
        [whole(32, 8, HID)],
        whole(32, 8, HID),
        shaped(32, 8, HID),
        cost(1, 520),
        (partner,),
        pieces,
    )
    moved = exchange(picked, ("y", "x")).reshape(BUNDLE, HID)

    terms = call(
        terms_kernel,
        (4,),
        [
            lead_block(4, BUNDLE, HID),
            whole(FEAT, HID),
            whole(FEAT, HID),
            whole(FEAT, HID),
        ],
        pl.BlockSpec((4, 2, CAP, 2 * FEAT), lambda i, coords: (0, i, 0, 0)),
        shaped(4, 8, CAP, 2 * FEAT),
        cost(1800, 8000),
        (coords,),
        in_hbm(own_acts),
        gate,
        up,
        down,
    )
    new_acts = lax.all_gather(moved, ("z", "core"), tiled=True).reshape(CHUNKS, BUNDLE, HID)

    returned = exchange(terms.reshape(4, 8 * CAP, 2 * FEAT), "x")
    merged = call(
        merge_kernel,
        (4,),
        [
            pl.BlockSpec((2, None, TOK, 128), lambda i, held, coords: (i, coords[1], 0, 3)),
            pl.BlockSpec((4, HALF, 2 * FEAT), lambda i, held, coords: (0, i, 0)),
        ],
        lead_block(PAIR, 2 * FEAT),
        shaped(8 * TOK, 2 * FEAT),
        cost(300, 3500),
        (held_before, coords),
        in_hbm(everyone.reshape(8, 4, TOK, 2 * WIDE)),
        returned,
    )
    home = exchange(merged.reshape(8, TOK, 2 * FEAT), "y")

    rows, scaled = call(
        new_rows_kernel,
        (4,),
        [lead_block(4, PAIR, 2 * WIDE)],
        (lead_block(4, HALF, FEAT), lead_block(4, HALF, FEAT)),
        (shaped(CHUNKS, HALF, FEAT), shaped(CHUNKS, HALF, FEAT)),
        cost(600, 6500),
        (held_before, partner, coords),
        in_hbm(everyone.reshape(CHUNKS, PAIR, 2 * WIDE)),
    )
    gate_grad, up_grad, down_grad = local(
        slab_grad_kernel,
        (shaped(FEAT, HID), shaped(FEAT, HID), shaped(FEAT, HID)),
        cost(1800, 8000),
        rows.reshape(ROWS, FEAT),
        scaled.reshape(ROWS, FEAT),
        new_acts,
    )

    total = jnp.sum(home.astype(F32), axis=0).astype(BF)
    return (total[:, :FEAT], total[:, FEAT:], gate_grad[None], up_grad[None], down_grad.T[None])


def solution(mesh):
    fine = Mesh(mesh.devices.reshape(8, 4, 8, 2), ("y", "x", "z", "core"))
    expert, dp = ("y", "x"), ("z", "core")
    slab = P(expert, dp, None)
    down = P(expert, None, dp)
    return jax.shard_map(
        body,
        mesh=fine,
        in_specs=(P(expert, dp), P(expert, dp), P(expert, None), P(expert, None), P(), P(), slab, slab, down),
        out_specs=(P(expert, dp), P(expert, dp), slab, slab, down),
        check_vma=False,
    )
```

```python
import jax
import jax.numpy as jnp
from jax import lax
from jax.experimental import pallas as pl
from jax.experimental.pallas import tpu as pltpu
from jax.sharding import Mesh, PartitionSpec as P

TOK = 64
CAP = 40
FEAT = 448
PACK = 2 * FEAT + TOK
HID = 512
PAIR = 2 * TOK
HALF = 2 * CAP
CHUNKS = 16
ROWS = CHUNKS * HALF
BUNDLE = 256
BF = jnp.bfloat16
F32 = jnp.float32


def dot(lhs, rhs):
    return jnp.dot(lhs, rhs, preferred_element_type=F32)


def dot_last(lhs, rhs):
    return lax.dot_general(lhs, rhs, (((1,), (1,)), ((), ())), preferred_element_type=F32)


def dot_first(lhs, rhs):
    return lax.dot_general(lhs, rhs, (((0,), (0,)), ((), ())), preferred_element_type=F32)


def as_matrix(hit):
    return jnp.where(hit, 1.0, 0.0).astype(BF)


def weight_rows(dense, experts):
    lane = lax.broadcasted_iota(jnp.int32, (8, TOK), 1)
    row = lax.broadcasted_iota(jnp.int32, (8, TOK), 0)
    hit = lane < 0
    for i, expert in enumerate(experts):
        hit = hit | ((row == i) & (lane == expert))
    return dot_last(as_matrix(hit), dense)


def slot_places(weights):
    count = weights.shape[1]
    routed = weights > 0.0
    source = lax.broadcasted_iota(jnp.int32, (count, count), 0)
    target = lax.broadcasted_iota(jnp.int32, (count, count), 1)
    earlier = (source < target) & ((source >> 6) == (target >> 6))
    position = dot(as_matrix(routed), as_matrix(earlier))
    group = lax.broadcasted_iota(jnp.int32, weights.shape, 1) >> 6
    return jnp.where(routed, position.astype(jnp.int32) + CAP * group, -1)


def one_hot(place, rows):
    return lax.broadcasted_iota(jnp.int32, (rows, place.shape[1]), 0) == place


def slot_weights(hit, weights):
    return jnp.sum(jnp.where(hit, weights, 0.0), axis=1, keepdims=True)


def two_slabs(weights, place, i):
    slot = lax.broadcasted_iota(jnp.int32, (HALF, TOK), 0)
    first = slot < CAP
    one, two = slice(2 * i, 2 * i + 1), slice(2 * i + 1, 2 * i + 2)
    hit = jnp.where(first, slot, slot - CAP) == jnp.where(first, place[one], place[two])
    return hit, jnp.where(hit, jnp.where(first, weights[one], weights[two]), 0.0)


def weights_of(names, ids_ref, probs_ref):
    return sum(jnp.where(ids_ref[k : k + 1] == names, probs_ref[k : k + 1].astype(F32), 0.0) for k in range(8))


def pack_kernel(tok_ref, cot_ref, ids_ref, probs_ref, packed_ref):
    names = lax.broadcasted_iota(jnp.int32, (TOK, TOK), 0)
    same = names == lax.broadcasted_iota(jnp.int32, (TOK, TOK), 1)
    dense = dot_first(weights_of(names, ids_ref, probs_ref).astype(BF), as_matrix(same)).astype(BF)
    packed_ref[...] = jnp.concatenate([tok_ref[...], cot_ref[...], dense], axis=1)


def slab_slots(held, ids_ref, probs_ref):
    slab = lax.broadcasted_iota(jnp.int32, (32, TOK), 0)
    expert = jnp.zeros((32, TOK), jnp.int32)
    for i in range(32):
        expert = jnp.where(slab == i, held[i] >> 1, expert)
    weights = weights_of(expert, ids_ref, probs_ref)
    return weights, slot_places(weights)


def slots_kernel(held, ids_ref, probs_ref, plain_ref, weighted_ref):
    weights, place = slab_slots(held, ids_ref, probs_ref)
    pairs = [two_slabs(weights, place, i) for i in range(CHUNKS)]
    token = lax.broadcasted_iota(jnp.int32, (TOK, TOK), 0)
    same = as_matrix(token == lax.broadcasted_iota(jnp.int32, (TOK, TOK), 1))
    plain = jnp.concatenate([as_matrix(hit) for hit, _ in pairs], axis=0)
    weighted = jnp.concatenate([factor.astype(BF) for _, factor in pairs], axis=0)
    plain_ref[...] = dot_last(same, plain).astype(BF)
    weighted_ref[...] = dot_last(same, weighted).astype(BF)


def rows_kernel(held, coords, packed_ref, after_ref, out_ref):
    weights = weight_rows(packed_ref[:, 2 * FEAT :], tuple(held[4 * coords[0] + i] >> 1 for i in range(4)))
    place = slot_places(weights)
    cot_lane = lax.broadcasted_iota(jnp.int32, (HALF, 2 * FEAT), 1) >= FEAT
    for i in range(4):
        hit = one_hot(place[i : i + 1], HALF)
        rows = dot(as_matrix(hit), packed_ref[:, : 2 * FEAT])
        out_ref[i] = (rows * jnp.where(cot_lane, slot_weights(hit, weights[i : i + 1]), 1.0)).astype(BF)


def products(rows_ref, gate_ref, up_ref, down_ref):
    count = rows_ref.shape[0]
    rows = rows_ref[...].reshape(count * HALF, 2 * FEAT)
    tok, scaled = rows[:, :FEAT], rows[:, FEAT:]
    three = dot(tok, gate_ref[...]), dot(tok, up_ref[...]), dot(scaled, down_ref[...])
    return [(slice(i * HID, (i + 1) * HID), part.reshape(count, HALF, HID)) for i, part in enumerate(three)]


def send_kernel(coords, rows_ref, gate_ref, up_ref, down_ref, out_ref):
    for lanes, part in products(rows_ref, gate_ref, up_ref, down_ref):
        out_ref[:, :, lanes] = part.astype(BF)


def keep_kernel(coords, rows_ref, gate_ref, up_ref, down_ref, got_ref, out_ref):
    for lanes, part in products(rows_ref, gate_ref, up_ref, down_ref):
        out_ref[:, :, lanes] = (part + got_ref[:, :, lanes].astype(F32)).astype(BF)


def activation_kernel(coords, sums_ref, after_ref, out_ref):
    sums = sums_ref[...].astype(F32)
    gate, up, grad = sums[:, :HID], sums[:, HID : 2 * HID], sums[:, 2 * HID :]
    sig = jax.nn.sigmoid(gate)
    activated = gate * sig
    out_ref[0:HALF] = (activated * up).astype(BF)
    out_ref[HALF : 2 * HALF] = (grad * up * sig * (1.0 + gate * (1.0 - sig))).astype(BF)
    out_ref[2 * HALF : 3 * HALF] = (grad * activated).astype(BF)
    out_ref[3 * HALF :] = jnp.zeros((BUNDLE - 3 * HALF, HID), BF)


def pick_kernel(partner, pieces_ref, out_ref):
    for j in range(32):
        out_ref[j] = pieces_ref[partner[j]]


def bundle_part(acts_ref, part):
    picked = acts_ref[:, part * HALF : (part + 1) * HALF, :]
    return picked.reshape(picked.shape[0] * HALF, HID)


def terms_kernel(coords, acts_ref, gate_ref, up_ref, down_ref, out_ref):
    out = dot_last(bundle_part(acts_ref, 0), down_ref[...])
    back = dot_last(bundle_part(acts_ref, 1), gate_ref[...]) + dot_last(bundle_part(acts_ref, 2), up_ref[...])
    both = jnp.concatenate([out, back], axis=1)
    for i in range(out_ref.shape[0]):
        out_ref[i, 0] = both[i * CAP : (i + 1) * CAP].astype(BF)


def merge_kernel(plain_ref, weighted_ref, rows_ref, out_ref, back_ref):
    out_ref[...] = dot(weighted_ref[...], rows_ref[...])[:, :FEAT].astype(BF)
    back_ref[...] = dot(plain_ref[...], rows_ref[...])[:, FEAT:].astype(BF)


def slab_grad_kernel(rows_ref, acts_ref, gate_ref, up_ref, down_ref):
    rows = rows_ref[:, :FEAT]
    gate_ref[...] = dot_first(rows, bundle_part(acts_ref, 1)).astype(BF)
    up_ref[...] = dot_first(rows, bundle_part(acts_ref, 2)).astype(BF)
    down_ref[...] = dot_first(rows_ref[:, FEAT:], bundle_part(acts_ref, 0)).astype(BF)


def shaped(*shape):
    return jax.ShapeDtypeStruct(shape, BF)


def params():
    return pltpu.CompilerParams(vmem_limit_bytes=32 * 1024 * 1024)


def cost(mflop, kbytes):
    return pl.CostEstimate(flops=mflop * 1_000_000, bytes_accessed=kbytes * 1000, transcendentals=0)


def call(kernel, grid, in_specs, out_specs, out_shape, estimate, scalars, *operands):
    return pl.pallas_call(
        kernel,
        grid_spec=pltpu.PrefetchScalarGridSpec(
            num_scalar_prefetch=len(scalars), grid=grid, in_specs=in_specs, out_specs=out_specs
        ),
        out_shape=out_shape,
        compiler_params=params(),
        cost_estimate=estimate,
    )(*scalars, *operands)


def local(kernel, out_shape, estimate, *operands):
    return pl.pallas_call(kernel, out_shape=out_shape, compiler_params=params(), cost_estimate=estimate)(*operands)


def whole(*shape):
    return pl.BlockSpec(shape, lambda i, *scalars: (0,) * len(shape))


def lead_block(*shape):
    return pl.BlockSpec(shape, lambda i, *scalars: (i,) + (0,) * (len(shape) - 1))


def core_half(count, rows, lanes, mine):
    if mine:
        return pl.BlockSpec((count, None, rows, lanes), lambda i, coords: (i, coords[2], 0, 0))
    return pl.BlockSpec((count, None, rows, lanes), lambda i, coords: (i, 1 - coords[2], 0, 0))


ANYWHERE = pl.BlockSpec(memory_space=pl.ANY)


def in_hbm(value):
    return pltpu.with_memory_space_constraint(value, pltpu.HBM)


def swap(value):
    return lax.ppermute(value, "core", [(0, 1), (1, 0)])


def exchange(value, axes):
    return lax.all_to_all(value, axes, split_axis=0, concat_axis=0, tiled=True)


def body(tokens, cotangent, expert_ids, route_probs, held_before, partner, gate_slabs, up_slabs, down_slabs):
    gate, up, down = gate_slabs[0], up_slabs[0], down_slabs[0].T
    coords = jnp.stack([lax.axis_index("y"), lax.axis_index("x"), lax.axis_index("core")]).astype(jnp.int32)

    ids, probs = expert_ids.T, route_probs.T
    packed = local(
        pack_kernel,
        shaped(TOK, PACK),
        cost(10, 300),
        in_hbm(tokens),
        in_hbm(cotangent),
        in_hbm(ids),
        in_hbm(probs),
    )
    column = lax.all_gather(packed, "y", tiled=True)

    def slab_rows(held, after):
        sent = call(
            rows_kernel,
            (4,),
            [lead_block(PAIR, PACK), ANYWHERE],
            pl.BlockSpec((4, HALF, 2 * FEAT), lambda i, held, coords: (0, i, 0)),
            pltpu.HBM((4, 4 * HALF, 2 * FEAT), BF),
            cost(600, 3500),
            (held, coords),
            column,
            in_hbm(after),
        )
        return exchange(sent, "x")

    own_rows = slab_rows(held_before, held_before)
    rows_view = own_rows.reshape(8, 2, HALF, 2 * FEAT)
    weight_specs = [whole(FEAT, HID), whole(FEAT, HID), whole(FEAT, HID)]
    sums_block = lead_block(4, HALF, 3 * HID)
    sending = call(
        send_kernel,
        (2,),
        [core_half(4, HALF, 2 * FEAT, False)] + weight_specs,
        sums_block,
        shaped(8, HALF, 3 * HID),
        cost(900, 4500),
        (coords,),
        rows_view,
        gate,
        up,
        down,
    )
    pairs = call(
        keep_kernel,
        (2,),
        [core_half(4, HALF, 2 * FEAT, True)] + weight_specs + [sums_block],
        sums_block,
        pltpu.HBM((8, HALF, 3 * HID), BF),
        cost(900, 6500),
        (coords,),
        rows_view,
        gate,
        up,
        down,
        swap(sending),
    )
    sums = lax.psum_scatter(pairs.reshape(8 * HALF, 3 * HID), "z", scatter_dimension=0, tiled=True)
    new_rows = slab_rows(jnp.take(held_before, partner), pairs)
    acts = call(
        activation_kernel,
        (1,),
        [whole(HALF, 3 * HID), ANYWHERE],
        whole(BUNDLE, HID),
        shaped(BUNDLE, HID),
        cost(3, 500),
        (coords,),
        sums,
        in_hbm(new_rows),
    )

    own_acts = lax.all_gather(acts, ("z", "core"), tiled=True).reshape(CHUNKS, BUNDLE, HID)
    pieces = exchange(acts.reshape(32, 8, HID), ("y", "x"))
    picked = call(
        pick_kernel,
        (1,),
        [whole(32, 8, HID)],
        whole(32, 8, HID),
        shaped(32, 8, HID),
        cost(1, 520),
        (partner,),
        pieces,
    )
    moved = exchange(picked, ("y", "x")).reshape(BUNDLE, HID)

    terms = call(
        terms_kernel,
        (4,),
        [
            lead_block(4, BUNDLE, HID),
            whole(FEAT, HID),
            whole(FEAT, HID),
            whole(FEAT, HID),
        ],
        pl.BlockSpec((8, 1, CAP, 2 * FEAT), lambda i, coords: (0, i, 0, 0)),
        pltpu.HBM((8, 4, CAP, 2 * FEAT), BF),
        cost(1800, 8000),
        (coords,),
        in_hbm(own_acts),
        gate,
        up,
        down,
    )
    new_acts = lax.all_gather(moved, ("z", "core"), tiled=True).reshape(CHUNKS, BUNDLE, HID)

    plain, weighted = call(
        slots_kernel,
        (1,),
        [whole(8, TOK), whole(8, TOK)],
        (whole(TOK, ROWS), whole(TOK, ROWS)),
        (shaped(TOK, ROWS), shaped(TOK, ROWS)),
        cost(20, 400),
        (held_before,),
        ids,
        probs,
    )
    layer_out, token_grad = local(
        merge_kernel,
        (shaped(TOK, FEAT), shaped(TOK, FEAT)),
        cost(300, 2400),
        plain,
        weighted,
        exchange(terms.reshape(32, CAP, 2 * FEAT), ("y", "x")).reshape(ROWS, 2 * FEAT),
    )

    gate_grad, up_grad, down_grad = local(
        slab_grad_kernel,
        (shaped(FEAT, HID), shaped(FEAT, HID), shaped(FEAT, HID)),
        cost(1800, 8000),
        new_rows.reshape(ROWS, 2 * FEAT),
        new_acts,
    )

    return (layer_out, token_grad, gate_grad[None], up_grad[None], down_grad.T[None])


def solution(mesh):
    fine = Mesh(mesh.devices.reshape(8, 4, 8, 2), ("y", "x", "z", "core"))
    expert, dp = ("y", "x"), ("z", "core")
    slab = P(expert, dp, None)
    down = P(expert, None, dp)
    return jax.shard_map(
        body,
        mesh=fine,
        in_specs=(P(expert, dp), P(expert, dp), P(expert, None), P(expert, None), P(), P(), slab, slab, down),
        out_specs=(P(expert, dp), P(expert, dp), slab, slab, down),
        check_vma=False,
    )
```

```python
import jax
import jax.numpy as jnp
from jax import lax
from jax.experimental import pallas as pl
from jax.experimental.pallas import tpu as pltpu
from jax.sharding import Mesh, PartitionSpec as P

TOK = 64
CAP = 40
FEAT = 448
PACK = 2 * FEAT + TOK
HID = 512
PAIR = 2 * TOK
HALF = 2 * CAP
CHUNKS = 16
ROWS = CHUNKS * HALF
BUNDLE = 256
BF = jnp.bfloat16
F32 = jnp.float32


def dot(lhs, rhs):
    return jnp.dot(lhs, rhs, preferred_element_type=F32)


def dot_last(lhs, rhs):
    return lax.dot_general(lhs, rhs, (((1,), (1,)), ((), ())), preferred_element_type=F32)


def dot_first(lhs, rhs):
    return lax.dot_general(lhs, rhs, (((0,), (0,)), ((), ())), preferred_element_type=F32)


def as_matrix(hit):
    return jnp.where(hit, 1.0, 0.0).astype(BF)


def weight_rows(dense, experts):
    lane = lax.broadcasted_iota(jnp.int32, (8, TOK), 1)
    row = lax.broadcasted_iota(jnp.int32, (8, TOK), 0)
    hit = lane < 0
    for i, expert in enumerate(experts):
        hit = hit | ((row == i) & (lane == expert))
    return dot_last(as_matrix(hit), dense)


def slot_places(weights):
    count = weights.shape[1]
    routed = weights > 0.0
    source = lax.broadcasted_iota(jnp.int32, (count, count), 0)
    target = lax.broadcasted_iota(jnp.int32, (count, count), 1)
    earlier = (source < target) & ((source >> 6) == (target >> 6))
    position = dot(as_matrix(routed), as_matrix(earlier))
    group = lax.broadcasted_iota(jnp.int32, weights.shape, 1) >> 6
    return jnp.where(routed, position.astype(jnp.int32) + CAP * group, -1)


def one_hot(place, rows):
    return lax.broadcasted_iota(jnp.int32, (rows, place.shape[1]), 0) == place


def slot_weights(hit, weights):
    return jnp.sum(jnp.where(hit, weights, 0.0), axis=1, keepdims=True)


def two_slabs(weights, place, i):
    slot = lax.broadcasted_iota(jnp.int32, (HALF, TOK), 0)
    first = slot < CAP
    one, two = slice(2 * i, 2 * i + 1), slice(2 * i + 1, 2 * i + 2)
    hit = jnp.where(first, slot, slot - CAP) == jnp.where(first, place[one], place[two])
    return hit, jnp.where(hit, jnp.where(first, weights[one], weights[two]), 0.0)


def weights_of(names, ids_ref, probs_ref):
    return sum(jnp.where(ids_ref[k : k + 1] == names, probs_ref[k : k + 1].astype(F32), 0.0) for k in range(8))


def pack_kernel(tok_ref, cot_ref, ids_ref, probs_ref, packed_ref):
    names = lax.broadcasted_iota(jnp.int32, (TOK, TOK), 0)
    same = names == lax.broadcasted_iota(jnp.int32, (TOK, TOK), 1)
    dense = dot_first(weights_of(names, ids_ref, probs_ref).astype(BF), as_matrix(same)).astype(BF)
    packed_ref[...] = jnp.concatenate([tok_ref[...], cot_ref[...], dense], axis=1)


def slab_slots(held, ids_ref, probs_ref):
    slab = lax.broadcasted_iota(jnp.int32, (32, TOK), 0)
    expert = jnp.zeros((32, TOK), jnp.int32)
    for i in range(32):
        expert = jnp.where(slab == i, held[i % 8 * 4 + i // 8] >> 1, expert)
    weights = weights_of(expert, ids_ref, probs_ref)
    return weights, slot_places(weights)


def slots_kernel(held, ids_ref, probs_ref, plain_ref, weighted_ref):
    weights, place = slab_slots(held, ids_ref, probs_ref)
    pairs = [two_slabs(weights, place, i) for i in range(CHUNKS)]
    token = lax.broadcasted_iota(jnp.int32, (TOK, TOK), 0)
    same = as_matrix(token == lax.broadcasted_iota(jnp.int32, (TOK, TOK), 1))
    plain = jnp.concatenate([as_matrix(hit) for hit, _ in pairs], axis=0)
    weighted = jnp.concatenate([factor.astype(BF) for _, factor in pairs], axis=0)
    plain_ref[...] = dot_last(same, plain).astype(BF)
    weighted_ref[...] = dot_last(same, weighted).astype(BF)


def rows_kernel(held, coords, packed_ref, after_ref, out_ref):
    weights = weight_rows(packed_ref[:, 2 * FEAT :], tuple(held[4 * coords[0] + i] >> 1 for i in range(4)))
    place = slot_places(weights)
    cot_lane = lax.broadcasted_iota(jnp.int32, (HALF, 2 * FEAT), 1) >= FEAT
    for i in range(4):
        hit = one_hot(place[i : i + 1], HALF)
        rows = dot(as_matrix(hit), packed_ref[:, : 2 * FEAT])
        out_ref[i, ...] = (rows * jnp.where(cot_lane, slot_weights(hit, weights[i : i + 1]), 1.0)).astype(BF).reshape(out_ref.shape[1:])


def products_kernel(coords, rows_ref, gate_ref, up_ref, down_ref, out_ref):
    count = rows_ref.shape[0]
    rows = rows_ref[...].reshape(count * HALF, 2 * FEAT)
    tok, scaled = rows[:, :FEAT], rows[:, FEAT:]
    three = dot(tok, gate_ref[...]), dot(tok, up_ref[...]), dot(scaled, down_ref[...])
    for i, part in enumerate(three):
        out_ref[:, :, i * HID : (i + 1) * HID] = part.astype(BF).reshape(count, HALF, HID)


def add_kernel(coords, own_ref, got_ref, out_ref):
    out_ref[...] = (own_ref[...].astype(F32) + got_ref[...].astype(F32)).astype(BF)


def activation_kernel(coords, sums_ref, after_ref, three_ref, out_ref):
    sums = sums_ref[...].astype(F32)
    gate, up, grad = sums[:, :HID], sums[:, HID : 2 * HID], sums[:, 2 * HID :]
    sig = jax.nn.sigmoid(gate)
    activated = gate * sig
    parts = activated * up, grad * up * sig * (1.0 + gate * (1.0 - sig)), grad * activated
    for i, part in enumerate(parts):
        three_ref[i * HALF : (i + 1) * HALF] = part.astype(BF)
        out_ref[i * HALF : (i + 1) * HALF] = part.astype(BF)
    out_ref[3 * HALF :] = jnp.zeros((BUNDLE - 3 * HALF, HID), BF)


def pick_kernel(partner, pieces_ref, out_ref):
    for j in range(32):
        out_ref[j] = pieces_ref[partner[j]]


def bundle_part(acts_ref, part):
    picked = acts_ref[:, part * HALF : (part + 1) * HALF, :]
    return picked.reshape(picked.shape[0] * HALF, HID)


def terms_kernel(coords, acts_ref, gate_ref, up_ref, down_ref, out_ref):
    out = dot_last(bundle_part(acts_ref, 0), down_ref[...])
    back = dot_last(bundle_part(acts_ref, 1), gate_ref[...]) + dot_last(bundle_part(acts_ref, 2), up_ref[...])
    out_ref[...] = jnp.concatenate([out, back], axis=1).astype(BF)


def merge_kernel(plain_ref, weighted_ref, rows_ref, out_ref, back_ref):
    out_ref[...] = dot(weighted_ref[...], rows_ref[...])[:, :FEAT].astype(BF)
    back_ref[...] = dot(plain_ref[...], rows_ref[...])[:, FEAT:].astype(BF)


def slab_grad_kernel(rows_ref, acts_ref, gate_ref, up_ref, down_ref):
    rows = rows_ref[:, :FEAT]
    gate_ref[...] = dot_first(rows, bundle_part(acts_ref, 1)).astype(BF)
    up_ref[...] = dot_first(rows, bundle_part(acts_ref, 2)).astype(BF)
    down_ref[...] = dot_first(rows_ref[:, FEAT:], bundle_part(acts_ref, 0)).astype(BF)


def shaped(*shape):
    return jax.ShapeDtypeStruct(shape, BF)


def params():
    return pltpu.CompilerParams(vmem_limit_bytes=32 * 1024 * 1024)


def cost(mflop, kbytes):
    return pl.CostEstimate(flops=mflop * 1_000_000, bytes_accessed=kbytes * 1000, transcendentals=0)


def call(kernel, grid, in_specs, out_specs, out_shape, estimate, scalars, *operands):
    return pl.pallas_call(
        kernel,
        grid_spec=pltpu.PrefetchScalarGridSpec(
            num_scalar_prefetch=len(scalars), grid=grid, in_specs=in_specs, out_specs=out_specs
        ),
        out_shape=out_shape,
        compiler_params=params(),
        cost_estimate=estimate,
    )(*scalars, *operands)


def local(kernel, out_shape, estimate, *operands):
    return pl.pallas_call(kernel, out_shape=out_shape, compiler_params=params(), cost_estimate=estimate)(*operands)


def whole(*shape):
    return pl.BlockSpec(shape, lambda i, *scalars: (0,) * len(shape))


def lead_block(*shape):
    return pl.BlockSpec(shape, lambda i, *scalars: (i,) + (0,) * (len(shape) - 1))


def core_half(count, rows, lanes, mine):
    if mine:
        return pl.BlockSpec((count, None, rows, lanes), lambda i, coords: (i, coords[2], 0, 0))
    return pl.BlockSpec((count, None, rows, lanes), lambda i, coords: (i, 1 - coords[2], 0, 0))


ANYWHERE = pl.BlockSpec(memory_space=pl.ANY)


def in_hbm(value):
    return pltpu.with_memory_space_constraint(value, pltpu.HBM)


def swap(value):
    return lax.ppermute(value, "core", [(0, 1), (1, 0)])


def exchange(value, axes):
    return lax.all_to_all(value, axes, split_axis=0, concat_axis=0, tiled=True)


def body(tokens, cotangent, expert_ids, route_probs, held_before, partner, gate_slabs, up_slabs, down_slabs):
    gate, up, down = gate_slabs[0], up_slabs[0], down_slabs[0].T
    coords = jnp.stack([lax.axis_index("y"), lax.axis_index("x"), lax.axis_index("core")]).astype(jnp.int32)

    ids, probs = expert_ids.T, route_probs.T
    packed = local(
        pack_kernel,
        shaped(TOK, PACK),
        cost(10, 300),
        in_hbm(tokens),
        in_hbm(cotangent),
        in_hbm(ids),
        in_hbm(probs),
    )
    column = lax.all_gather(packed, "y", tiled=True)

    def slab_rows(held, after, block, shape):
        return call(
            rows_kernel,
            (4,),
            [lead_block(PAIR, PACK), ANYWHERE],
            block,
            pltpu.HBM(shape, BF),
            cost(600, 3500),
            (held, coords),
            column,
            in_hbm(after),
        )

    in_pairs = pl.BlockSpec((4, 1, HALF, 2 * FEAT), lambda i, *scalars: (0, i, 0, 0))
    sent = slab_rows(held_before, held_before, in_pairs, (4, 4, HALF, 2 * FEAT))
    rows_view = exchange(sent.reshape(4, 4 * HALF, 2 * FEAT), "x").reshape(8, 2, HALF, 2 * FEAT)

    def products(mine):
        return call(
            products_kernel,
            (2,),
            [core_half(4, HALF, 2 * FEAT, mine)] + [whole(FEAT, HID)] * 3,
            lead_block(4, HALF, 3 * HID),
            shaped(8, HALF, 3 * HID),
            cost(900, 4500),
            (coords,),
            rows_view,
            gate,
            up,
            down,
        )

    got = swap(products(False))
    pairs = call(
        add_kernel,
        (4,),
        [lead_block(2, HALF, 3 * HID)] * 2,
        lead_block(2, HALF, 3 * HID),
        pltpu.HBM((8, HALF, 3 * HID), BF),
        cost(1, 6000),
        (coords,),
        products(True),
        got,
    )
    sums = lax.psum_scatter(pairs.reshape(8 * HALF, 3 * HID), "z", scatter_dimension=0, tiled=True)
    new_sent = slab_rows(jnp.take(held_before, partner), pairs, in_pairs, (4, 4, HALF, 2 * FEAT))
    new_rows = exchange(new_sent.reshape(4, 4 * HALF, 2 * FEAT), "x")
    three, acts = call(
        activation_kernel,
        (1,),
        [whole(HALF, 3 * HID), ANYWHERE],
        (whole(3 * HALF, HID), whole(BUNDLE, HID)),
        (shaped(3 * HALF, HID), shaped(BUNDLE, HID)),
        cost(3, 500),
        (coords,),
        in_hbm(sums),
        in_hbm(new_rows),
    )

    own_acts = lax.all_gather(three, ("z", "core"), tiled=True).reshape(CHUNKS, 3 * HALF, HID)
    pieces = exchange(acts.reshape(32, 8, HID), ("y", "x"))
    picked = call(
        pick_kernel,
        (1,),
        [whole(32, 8, HID)],
        whole(32, 8, HID),
        shaped(32, 8, HID),
        cost(1, 520),
        (partner,),
        pieces,
    )
    moved = exchange(picked, ("y", "x")).reshape(BUNDLE, HID)

    terms = call(
        terms_kernel,
        (2,),
        [
            lead_block(8, 3 * HALF, HID),
            whole(FEAT, HID),
            whole(FEAT, HID),
            whole(FEAT, HID),
        ],
        lead_block(ROWS // 2, 2 * FEAT),
        pltpu.HBM((ROWS, 2 * FEAT), BF),
        cost(1800, 8000),
        (coords,),
        in_hbm(own_acts),
        gate,
        up,
        down,
    )
    new_acts = lax.all_gather(moved[: 3 * HALF], ("z", "core"), tiled=True).reshape(CHUNKS, 3 * HALF, HID)

    plain, weighted = call(
        slots_kernel,
        (1,),
        [whole(8, TOK), whole(8, TOK)],
        (whole(TOK, ROWS), whole(TOK, ROWS)),
        (shaped(TOK, ROWS), shaped(TOK, ROWS)),
        cost(20, 400),
        (held_before,),
        ids,
        probs,
    )
    layer_out, token_grad = local(
        merge_kernel,
        (shaped(TOK, FEAT), shaped(TOK, FEAT)),
        cost(300, 2400),
        plain,
        weighted,
        exchange(terms.reshape(32, CAP, 2 * FEAT), ("x", "y")).reshape(ROWS, 2 * FEAT),
    )

    gate_grad, up_grad, down_grad = local(
        slab_grad_kernel,
        (shaped(FEAT, HID), shaped(FEAT, HID), shaped(FEAT, HID)),
        cost(1800, 8000),
        in_hbm(new_rows.reshape(ROWS, 2 * FEAT)),
        in_hbm(new_acts),
    )

    return (layer_out, token_grad, gate_grad[None], up_grad[None], down_grad.T[None])


def solution(mesh):
    fine = Mesh(mesh.devices.reshape(8, 4, 8, 2), ("y", "x", "z", "core"))
    expert, dp = ("y", "x"), ("z", "core")
    slab = P(expert, dp, None)
    down = P(expert, None, dp)
    return jax.shard_map(
        body,
        mesh=fine,
        in_specs=(P(expert, dp), P(expert, dp), P(expert, None), P(expert, None), P(), P(), slab, slab, down),
        out_specs=(P(expert, dp), P(expert, dp), slab, slab, down),
        check_vma=False,
    )
```

```python
import jax
import jax.numpy as jnp
from jax import lax
from jax.experimental import pallas as pl
from jax.experimental.pallas import tpu as pltpu
from jax.sharding import Mesh, PartitionSpec as P

TOK = 64
CAP = 40
FEAT = 448
PACK = 2 * FEAT + TOK
HID = 512
PAIR = 2 * TOK
HALF = 2 * CAP
CHUNKS = 16
ROWS = CHUNKS * HALF
BUNDLE = 256
BF = jnp.bfloat16
F32 = jnp.float32


def dot(lhs, rhs):
    return jnp.dot(lhs, rhs, preferred_element_type=F32)


def dot_last(lhs, rhs):
    return lax.dot_general(lhs, rhs, (((1,), (1,)), ((), ())), preferred_element_type=F32)


def dot_first(lhs, rhs):
    return lax.dot_general(lhs, rhs, (((0,), (0,)), ((), ())), preferred_element_type=F32)


def as_matrix(hit):
    return jnp.where(hit, 1.0, 0.0).astype(BF)


def weight_rows(dense, experts):
    lane = lax.broadcasted_iota(jnp.int32, (8, TOK), 1)
    row = lax.broadcasted_iota(jnp.int32, (8, TOK), 0)
    hit = lane < 0
    for i, expert in enumerate(experts):
        hit = hit | ((row == i) & (lane == expert))
    return dot_last(as_matrix(hit), dense)


def slot_places(weights):
    count = weights.shape[1]
    routed = weights > 0.0
    source = lax.broadcasted_iota(jnp.int32, (count, count), 0)
    target = lax.broadcasted_iota(jnp.int32, (count, count), 1)
    earlier = (source < target) & ((source >> 6) == (target >> 6))
    position = dot(as_matrix(routed), as_matrix(earlier))
    group = lax.broadcasted_iota(jnp.int32, weights.shape, 1) >> 6
    return jnp.where(routed, position.astype(jnp.int32) + CAP * group, -1)


def one_hot(place, rows):
    return lax.broadcasted_iota(jnp.int32, (rows, place.shape[1]), 0) == place


def slot_weights(hit, weights):
    return jnp.sum(jnp.where(hit, weights, 0.0), axis=1, keepdims=True)


def two_slabs(weights, place, i):
    slot = lax.broadcasted_iota(jnp.int32, (HALF, TOK), 0)
    first = slot < CAP
    one, two = slice(2 * i, 2 * i + 1), slice(2 * i + 1, 2 * i + 2)
    hit = jnp.where(first, slot, slot - CAP) == jnp.where(first, place[one], place[two])
    return hit, jnp.where(hit, jnp.where(first, weights[one], weights[two]), 0.0)


def weights_of(names, ids_ref, probs_ref):
    return sum(jnp.where(ids_ref[k : k + 1] == names, probs_ref[k : k + 1].astype(F32), 0.0) for k in range(8))


def pack_kernel(tok_ref, cot_ref, ids_ref, probs_ref, packed_ref):
    names = lax.broadcasted_iota(jnp.int32, (TOK, TOK), 0)
    same = names == lax.broadcasted_iota(jnp.int32, (TOK, TOK), 1)
    dense = dot_first(weights_of(names, ids_ref, probs_ref).astype(BF), as_matrix(same)).astype(BF)
    packed_ref[...] = jnp.concatenate([tok_ref[...], cot_ref[...], dense], axis=1)


def slab_slots(held, ids_ref, probs_ref):
    slab = lax.broadcasted_iota(jnp.int32, (32, TOK), 0)
    expert = jnp.zeros((32, TOK), jnp.int32)
    for i in range(32):
        expert = jnp.where(slab == i, held[i % 8 * 4 + i // 8] >> 1, expert)
    weights = weights_of(expert, ids_ref, probs_ref)
    return weights, slot_places(weights)


def slots_kernel(held, ids_ref, probs_ref, plain_ref, weighted_ref):
    weights, place = slab_slots(held, ids_ref, probs_ref)
    pairs = [two_slabs(weights, place, i) for i in range(CHUNKS)]
    token = lax.broadcasted_iota(jnp.int32, (TOK, TOK), 0)
    same = as_matrix(token == lax.broadcasted_iota(jnp.int32, (TOK, TOK), 1))
    plain = jnp.concatenate([as_matrix(hit) for hit, _ in pairs], axis=0)
    weighted = jnp.concatenate([factor.astype(BF) for _, factor in pairs], axis=0)
    plain_ref[...] = dot_last(same, plain).astype(BF)
    weighted_ref[...] = dot_last(same, weighted).astype(BF)


def rows_kernel(held, coords, packed_ref, after_ref, out_ref):
    experts = tuple(held[4 * coords[0] + i] >> 1 for i in range(4))
    cot_lane = lax.broadcasted_iota(jnp.int32, (HALF, 2 * FEAT), 1) >= FEAT
    for pair in range(out_ref.shape[1]):
        packed = packed_ref[pair * PAIR : (pair + 1) * PAIR]
        weights = weight_rows(packed[:, 2 * FEAT :], experts)
        place = slot_places(weights)
        hits = [one_hot(place[i : i + 1], HALF) for i in range(4)]
        rows = dot(jnp.concatenate([as_matrix(hit) for hit in hits], axis=0), packed[:, : 2 * FEAT])
        for i, hit in enumerate(hits):
            factor = jnp.where(cot_lane, slot_weights(hit, weights[i : i + 1]), 1.0)
            out_ref[i, pair] = (rows[i * HALF : (i + 1) * HALF] * factor).astype(BF)


def products_kernel(coords, rows_ref, gate_ref, up_ref, down_ref, out_ref):
    count = rows_ref.shape[0]
    rows = rows_ref[...].reshape(count * HALF, 2 * FEAT)
    tok, scaled = rows[:, :FEAT], rows[:, FEAT:]
    three = dot(tok, gate_ref[...]), dot(tok, up_ref[...]), dot(scaled, down_ref[...])
    for i, part in enumerate(three):
        out_ref[:, :, i * HID : (i + 1) * HID] = part.astype(BF).reshape(count, HALF, HID)


def add_kernel(coords, own_ref, got_ref, out_ref):
    out_ref[...] = (own_ref[...].astype(F32) + got_ref[...].astype(F32)).astype(BF)


def activation_kernel(coords, sums_ref, after_ref, three_ref, out_ref):
    sums = sums_ref[...].astype(F32)
    gate, up, grad = sums[:, :HID], sums[:, HID : 2 * HID], sums[:, 2 * HID :]
    sig = jax.nn.sigmoid(gate)
    activated = gate * sig
    parts = activated * up, grad * up * sig * (1.0 + gate * (1.0 - sig)), grad * activated
    for i, part in enumerate(parts):
        three_ref[i * HALF : (i + 1) * HALF] = part.astype(BF)
        out_ref[i * HALF : (i + 1) * HALF] = part.astype(BF)
    out_ref[3 * HALF :] = jnp.zeros((BUNDLE - 3 * HALF, HID), BF)


def pick_kernel(partner, pieces_ref, out_ref):
    for j in range(32):
        out_ref[j] = pieces_ref[partner[j]]


def bundle_part(acts_ref, part):
    picked = acts_ref[:, part * HALF : (part + 1) * HALF, :]
    return picked.reshape(picked.shape[0] * HALF, HID)


def terms_kernel(coords, acts_ref, gate_ref, up_ref, down_ref, out_ref):
    out = dot_last(bundle_part(acts_ref, 0), down_ref[...])
    back = dot_last(bundle_part(acts_ref, 1), gate_ref[...]) + dot_last(bundle_part(acts_ref, 2), up_ref[...])
    out_ref[...] = jnp.concatenate([out, back], axis=1).astype(BF)


def merge_kernel(plain_ref, weighted_ref, rows_ref, out_ref, back_ref):
    out_ref[...] = dot(weighted_ref[...], rows_ref[...])[:, :FEAT].astype(BF)
    back_ref[...] = dot(plain_ref[...], rows_ref[...])[:, FEAT:].astype(BF)


def slab_grad_kernel(rows_ref, acts_ref, gate_ref, up_ref, down_ref):
    rows = rows_ref[:, :FEAT]
    gate_ref[...] = dot_first(rows, bundle_part(acts_ref, 1)).astype(BF)
    up_ref[...] = dot_first(rows, bundle_part(acts_ref, 2)).astype(BF)
    down_ref[...] = dot_first(rows_ref[:, FEAT:], bundle_part(acts_ref, 0)).astype(BF)


def shaped(*shape):
    return jax.ShapeDtypeStruct(shape, BF)


def params():
    return pltpu.CompilerParams(vmem_limit_bytes=32 * 1024 * 1024)


def cost(mflop, kbytes):
    return pl.CostEstimate(flops=mflop * 1_000_000, bytes_accessed=kbytes * 1000, transcendentals=0)


def call(kernel, grid, in_specs, out_specs, out_shape, estimate, scalars, *operands):
    return pl.pallas_call(
        kernel,
        grid_spec=pltpu.PrefetchScalarGridSpec(
            num_scalar_prefetch=len(scalars), grid=grid, in_specs=in_specs, out_specs=out_specs
        ),
        out_shape=out_shape,
        compiler_params=params(),
        cost_estimate=estimate,
    )(*scalars, *operands)


def local(kernel, out_shape, estimate, *operands):
    return pl.pallas_call(kernel, out_shape=out_shape, compiler_params=params(), cost_estimate=estimate)(*operands)


def whole(*shape):
    return pl.BlockSpec(shape, lambda i, *scalars: (0,) * len(shape))


def lead_block(*shape):
    return pl.BlockSpec(shape, lambda i, *scalars: (i,) + (0,) * (len(shape) - 1))


def core_half(count, rows, lanes, mine):
    if mine:
        return pl.BlockSpec((count, None, rows, lanes), lambda i, coords: (i, coords[2], 0, 0))
    return pl.BlockSpec((count, None, rows, lanes), lambda i, coords: (i, 1 - coords[2], 0, 0))


ANYWHERE = pl.BlockSpec(memory_space=pl.ANY)


def in_hbm(value):
    return pltpu.with_memory_space_constraint(value, pltpu.HBM)


def swap(value):
    return lax.ppermute(value, "core", [(0, 1), (1, 0)])


def exchange(value, axes):
    return lax.all_to_all(value, axes, split_axis=0, concat_axis=0, tiled=True)


def body(tokens, cotangent, expert_ids, route_probs, held_before, partner, gate_slabs, up_slabs, down_slabs):
    gate, up, down = gate_slabs[0], up_slabs[0], down_slabs[0].T
    coords = jnp.stack([lax.axis_index("y"), lax.axis_index("x"), lax.axis_index("core")]).astype(jnp.int32)

    ids, probs = expert_ids.T, route_probs.T
    packed = local(
        pack_kernel,
        shaped(TOK, PACK),
        cost(10, 300),
        in_hbm(tokens),
        in_hbm(cotangent),
        in_hbm(ids),
        in_hbm(probs),
    )
    column = lax.all_gather(packed, "y", tiled=True)

    def slab_rows(held, after, shape):
        sent = call(
            rows_kernel,
            (2,),
            [lead_block(2 * PAIR, PACK), ANYWHERE],
            pl.BlockSpec((4, 2, HALF, 2 * FEAT), lambda i, *scalars: (0, i, 0, 0)),
            shape,
            cost(600, 3500),
            (held, coords),
            column,
            in_hbm(after),
        )
        return exchange(sent.reshape(4, 4 * HALF, 2 * FEAT), "x")

    sent_shape = (4, 4, HALF, 2 * FEAT)
    rows_view = slab_rows(held_before, held_before, shaped(*sent_shape)).reshape(8, 2, HALF, 2 * FEAT)

    def products(mine):
        return call(
            products_kernel,
            (2,),
            [core_half(4, HALF, 2 * FEAT, mine)] + [whole(FEAT, HID)] * 3,
            lead_block(4, HALF, 3 * HID),
            shaped(8, HALF, 3 * HID),
            cost(900, 4500),
            (coords,),
            rows_view,
            gate,
            up,
            down,
        )

    got = swap(products(False))
    pairs = call(
        add_kernel,
        (2,),
        [lead_block(4, HALF, 3 * HID)] * 2,
        lead_block(4, HALF, 3 * HID),
        pltpu.HBM((8, HALF, 3 * HID), BF),
        cost(1, 6000),
        (coords,),
        products(True),
        got,
    )
    sums = lax.psum_scatter(pairs.reshape(8 * HALF, 3 * HID), "z", scatter_dimension=0, tiled=True)
    new_rows = slab_rows(jnp.take(held_before, partner), pairs, pltpu.HBM(sent_shape, BF))
    three, acts = call(
        activation_kernel,
        (1,),
        [whole(HALF, 3 * HID), ANYWHERE],
        (whole(3 * HALF, HID), whole(BUNDLE, HID)),
        (shaped(3 * HALF, HID), shaped(BUNDLE, HID)),
        cost(3, 500),
        (coords,),
        in_hbm(sums),
        in_hbm(new_rows),
    )

    own_acts = lax.all_gather(three, ("z", "core"), tiled=True).reshape(CHUNKS, 3 * HALF, HID)
    pieces = exchange(acts.reshape(32, 8, HID), ("y", "x"))
    picked = call(
        pick_kernel,
        (1,),
        [whole(32, 8, HID)],
        whole(32, 8, HID),
        shaped(32, 8, HID),
        cost(1, 520),
        (partner,),
        pieces,
    )
    moved = exchange(picked, ("y", "x")).reshape(BUNDLE, HID)

    terms = call(
        terms_kernel,
        (2,),
        [
            lead_block(8, 3 * HALF, HID),
            whole(FEAT, HID),
            whole(FEAT, HID),
            whole(FEAT, HID),
        ],
        lead_block(ROWS // 2, 2 * FEAT),
        pltpu.HBM((ROWS, 2 * FEAT), BF),
        cost(1800, 8000),
        (coords,),
        in_hbm(own_acts),
        gate,
        up,
        down,
    )
    new_acts = lax.all_gather(moved[: 3 * HALF], ("z", "core"), tiled=True).reshape(CHUNKS, 3 * HALF, HID)

    plain, weighted = call(
        slots_kernel,
        (1,),
        [whole(8, TOK), whole(8, TOK)],
        (whole(TOK, ROWS), whole(TOK, ROWS)),
        (shaped(TOK, ROWS), shaped(TOK, ROWS)),
        cost(20, 400),
        (held_before,),
        ids,
        probs,
    )
    layer_out, token_grad = local(
        merge_kernel,
        (shaped(TOK, FEAT), shaped(TOK, FEAT)),
        cost(300, 2400),
        plain,
        weighted,
        exchange(terms.reshape(32, CAP, 2 * FEAT), ("x", "y")).reshape(ROWS, 2 * FEAT),
    )

    gate_grad, up_grad, down_grad = local(
        slab_grad_kernel,
        (shaped(FEAT, HID), shaped(FEAT, HID), shaped(FEAT, HID)),
        cost(1800, 8000),
        in_hbm(new_rows.reshape(ROWS, 2 * FEAT)),
        in_hbm(new_acts),
    )

    return (layer_out, token_grad, gate_grad[None], up_grad[None], down_grad.T[None])


def solution(mesh):
    fine = Mesh(mesh.devices.reshape(8, 4, 8, 2), ("y", "x", "z", "core"))
    expert, dp = ("y", "x"), ("z", "core")
    slab = P(expert, dp, None)
    down = P(expert, None, dp)
    return jax.shard_map(
        body,
        mesh=fine,
        in_specs=(P(expert, dp), P(expert, dp), P(expert, None), P(expert, None), P(), P(), slab, slab, down),
        out_specs=(P(expert, dp), P(expert, dp), slab, slab, down),
        check_vma=False,
    )
```

```python
import jax
import jax.numpy as jnp
from jax import lax
from jax.experimental import pallas as pl
from jax.experimental.pallas import tpu as pltpu
from jax.sharding import Mesh, PartitionSpec as P

TOK = 64
CAP = 40
FEAT = 448
PACK = 2 * FEAT + TOK
HID = 512
PAIR = 2 * TOK
HALF = 2 * CAP
CHUNKS = 16
ROWS = CHUNKS * HALF
BUNDLE = 256
BF = jnp.bfloat16
F32 = jnp.float32


def dot(lhs, rhs):
    return jnp.dot(lhs, rhs, preferred_element_type=F32)


def dot_last(lhs, rhs):
    return lax.dot_general(lhs, rhs, (((1,), (1,)), ((), ())), preferred_element_type=F32)


def dot_first(lhs, rhs):
    return lax.dot_general(lhs, rhs, (((0,), (0,)), ((), ())), preferred_element_type=F32)


def as_matrix(hit):
    return jnp.where(hit, 1.0, 0.0).astype(BF)


def weight_rows(dense, experts):
    lane = lax.broadcasted_iota(jnp.int32, (8, TOK), 1)
    row = lax.broadcasted_iota(jnp.int32, (8, TOK), 0)
    hit = lane < 0
    for i, expert in enumerate(experts):
        hit = hit | ((row == i) & (lane == expert))
    return dot_last(as_matrix(hit), dense)


def slot_places(weights):
    count = weights.shape[1]
    routed = weights > 0.0
    source = lax.broadcasted_iota(jnp.int32, (count, count), 0)
    target = lax.broadcasted_iota(jnp.int32, (count, count), 1)
    earlier = (source < target) & ((source >> 6) == (target >> 6))
    position = dot(as_matrix(routed), as_matrix(earlier))
    group = lax.broadcasted_iota(jnp.int32, weights.shape, 1) >> 6
    return jnp.where(routed, position.astype(jnp.int32) + CAP * group, -1)


def one_hot(place, rows):
    return lax.broadcasted_iota(jnp.int32, (rows, place.shape[1]), 0) == place


def slot_weights(hit, weights):
    return jnp.sum(jnp.where(hit, weights, 0.0), axis=1, keepdims=True)


def two_slabs(weights, place, i):
    slot = lax.broadcasted_iota(jnp.int32, (HALF, TOK), 0)
    first = slot < CAP
    one, two = slice(2 * i, 2 * i + 1), slice(2 * i + 1, 2 * i + 2)
    hit = jnp.where(first, slot, slot - CAP) == jnp.where(first, place[one], place[two])
    return hit, jnp.where(hit, jnp.where(first, weights[one], weights[two]), 0.0)


def weights_of(names, ids_ref, probs_ref):
    ids, probs = ids_ref[...], probs_ref[...].astype(F32)
    return sum(jnp.where(ids[k : k + 1] == names, probs[k : k + 1], 0.0) for k in range(8))


def pack_kernel(tok_ref, cot_ref, ids_ref, probs_ref, packed_ref):
    names = lax.broadcasted_iota(jnp.int32, (TOK, TOK), 0)
    same = names == lax.broadcasted_iota(jnp.int32, (TOK, TOK), 1)
    dense = dot_first(weights_of(names, ids_ref, probs_ref).astype(BF), as_matrix(same)).astype(BF)
    packed_ref[...] = jnp.concatenate([tok_ref[...], cot_ref[...], dense], axis=1)


def slab_slots(held, ids_ref, probs_ref):
    slab = lax.broadcasted_iota(jnp.int32, (32, TOK), 0)
    expert = jnp.zeros((32, TOK), jnp.int32)
    for i in range(32):
        expert = jnp.where(slab == i, held[i % 8 * 4 + i // 8] >> 1, expert)
    weights = weights_of(expert, ids_ref, probs_ref)
    return weights, slot_places(weights)


def slots_kernel(held, ids_ref, probs_ref, plain_ref, weighted_ref):
    weights, place = slab_slots(held, ids_ref, probs_ref)
    pairs = [two_slabs(weights, place, i) for i in range(CHUNKS)]
    token = lax.broadcasted_iota(jnp.int32, (TOK, TOK), 0)
    same = as_matrix(token == lax.broadcasted_iota(jnp.int32, (TOK, TOK), 1))
    plain = jnp.concatenate([as_matrix(hit) for hit, _ in pairs], axis=0)
    weighted = jnp.concatenate([factor.astype(BF) for _, factor in pairs], axis=0)
    plain_ref[...] = dot_last(same, plain).astype(BF)
    weighted_ref[...] = dot_last(same, weighted).astype(BF)


def rows_kernel(held, coords, packed_ref, after_ref, out_ref):
    experts = tuple(held[4 * coords[0] + i] >> 1 for i in range(4))
    cot_lane = lax.broadcasted_iota(jnp.int32, (HALF, 2 * FEAT), 1) >= FEAT
    for pair in range(out_ref.shape[1]):
        packed = packed_ref[pair * PAIR : (pair + 1) * PAIR]
        weights = weight_rows(packed[:, 2 * FEAT :], experts)
        place = slot_places(weights)
        hits = [one_hot(place[i : i + 1], HALF) for i in range(4)]
        rows = dot(jnp.concatenate([as_matrix(hit) for hit in hits], axis=0), packed[:, : 2 * FEAT])
        for i, hit in enumerate(hits):
            factor = jnp.where(cot_lane, slot_weights(hit, weights[i : i + 1]), 1.0)
            out_ref[i, pair] = (rows[i * HALF : (i + 1) * HALF] * factor).astype(BF)


def products_kernel(coords, rows_ref, gate_ref, up_ref, down_ref, out_ref):
    count = rows_ref.shape[0]
    rows = rows_ref[...].reshape(count * HALF, 2 * FEAT)
    tok, scaled = rows[:, :FEAT], rows[:, FEAT:]
    three = dot(tok, gate_ref[...]), dot(tok, up_ref[...]), dot(scaled, down_ref[...])
    for i, part in enumerate(three):
        out_ref[:, :, i * HID : (i + 1) * HID] = part.astype(BF).reshape(count, HALF, HID)


def add_kernel(coords, own_ref, got_ref, out_ref):
    out_ref[...] = (own_ref[...].astype(F32) + got_ref[...].astype(F32)).astype(BF)


def activation_kernel(coords, sums_ref, after_ref, three_ref, out_ref):
    sums = sums_ref[...].astype(F32)
    gate, up, grad = sums[:, :HID], sums[:, HID : 2 * HID], sums[:, 2 * HID :]
    sig = jax.nn.sigmoid(gate)
    activated = gate * sig
    parts = activated * up, grad * up * sig * (1.0 + gate * (1.0 - sig)), grad * activated
    for i, part in enumerate(parts):
        three_ref[i * HALF : (i + 1) * HALF] = part.astype(BF)
        out_ref[i * HALF : (i + 1) * HALF] = part.astype(BF)
    out_ref[3 * HALF :] = jnp.zeros((BUNDLE - 3 * HALF, HID), BF)


def pick_kernel(partner, pieces_ref, out_ref):
    for j in range(32):
        out_ref[j] = pieces_ref[partner[j]]


def bundle_part(acts_ref, part):
    picked = acts_ref[:, part * HALF : (part + 1) * HALF, :]
    return picked.reshape(picked.shape[0] * HALF, HID)


def terms_kernel(coords, acts_ref, gate_ref, up_ref, down_ref, out_ref):
    out = dot_last(bundle_part(acts_ref, 0), down_ref[...])
    back = dot_last(bundle_part(acts_ref, 1), gate_ref[...]) + dot_last(bundle_part(acts_ref, 2), up_ref[...])
    out_ref[...] = jnp.concatenate([out, back], axis=1).astype(BF)


def merge_kernel(plain_ref, weighted_ref, rows_ref, out_ref, back_ref):
    out_ref[...] = dot(weighted_ref[...], rows_ref[...])[:, :FEAT].astype(BF)
    back_ref[...] = dot(plain_ref[...], rows_ref[...])[:, FEAT:].astype(BF)


def slab_grad_kernel(rows_ref, acts_ref, gate_ref, up_ref, down_ref):
    rows = rows_ref[:, :FEAT]
    gate_ref[...] = dot_first(rows, bundle_part(acts_ref, 1)).astype(BF)
    up_ref[...] = dot_first(rows, bundle_part(acts_ref, 2)).astype(BF)
    down_ref[...] = dot_first(rows_ref[:, FEAT:], bundle_part(acts_ref, 0)).astype(BF)


def shaped(*shape):
    return jax.ShapeDtypeStruct(shape, BF)


def params():
    return pltpu.CompilerParams(vmem_limit_bytes=32 * 1024 * 1024)


def cost(mflop, kbytes):
    return pl.CostEstimate(flops=mflop * 1_000_000, bytes_accessed=kbytes * 1000, transcendentals=0)


def call(kernel, grid, in_specs, out_specs, out_shape, estimate, scalars, *operands):
    return pl.pallas_call(
        kernel,
        grid_spec=pltpu.PrefetchScalarGridSpec(
            num_scalar_prefetch=len(scalars), grid=grid, in_specs=in_specs, out_specs=out_specs
        ),
        out_shape=out_shape,
        compiler_params=params(),
        cost_estimate=estimate,
    )(*scalars, *operands)


def local(kernel, out_shape, estimate, *operands):
    return pl.pallas_call(kernel, out_shape=out_shape, compiler_params=params(), cost_estimate=estimate)(*operands)


def whole(*shape):
    return pl.BlockSpec(shape, lambda i, *scalars: (0,) * len(shape))


def lead_block(*shape):
    return pl.BlockSpec(shape, lambda i, *scalars: (i,) + (0,) * (len(shape) - 1))


def core_half(count, rows, lanes, mine):
    if mine:
        return pl.BlockSpec((count, None, rows, lanes), lambda i, coords: (i, coords[2], 0, 0))
    return pl.BlockSpec((count, None, rows, lanes), lambda i, coords: (i, 1 - coords[2], 0, 0))


ANYWHERE = pl.BlockSpec(memory_space=pl.ANY)


def in_hbm(value):
    return pltpu.with_memory_space_constraint(value, pltpu.HBM)


def swap(value):
    return lax.ppermute(value, "core", [(0, 1), (1, 0)])


def exchange(value, axes):
    return lax.all_to_all(value, axes, split_axis=0, concat_axis=0, tiled=True)


def body(tokens, cotangent, expert_ids, route_probs, held_before, partner, gate_slabs, up_slabs, down_slabs):
    gate, up, down = gate_slabs[0], up_slabs[0], down_slabs[0].T
    coords = jnp.stack([lax.axis_index("y"), lax.axis_index("x"), lax.axis_index("core")]).astype(jnp.int32)

    ids, probs = expert_ids.T, route_probs.T
    packed = local(
        pack_kernel,
        shaped(TOK, PACK),
        cost(10, 300),
        in_hbm(tokens),
        in_hbm(cotangent),
        in_hbm(ids),
        in_hbm(probs),
    )
    column = lax.all_gather(packed, "y", tiled=True)

    def slab_rows(held, after, shape):
        sent = call(
            rows_kernel,
            (2,),
            [lead_block(2 * PAIR, PACK), ANYWHERE],
            pl.BlockSpec((4, 2, HALF, 2 * FEAT), lambda i, *scalars: (0, i, 0, 0)),
            shape,
            cost(600, 3500),
            (held, coords),
            column,
            in_hbm(after),
        )
        return exchange(sent.reshape(4, 4 * HALF, 2 * FEAT), "x")

    sent_shape = (4, 4, HALF, 2 * FEAT)
    rows_view = slab_rows(held_before, held_before, shaped(*sent_shape)).reshape(8, 2, HALF, 2 * FEAT)

    def products(mine):
        return call(
            products_kernel,
            (2,),
            [core_half(4, HALF, 2 * FEAT, mine)] + [whole(FEAT, HID)] * 3,
            lead_block(4, HALF, 3 * HID),
            shaped(8, HALF, 3 * HID),
            cost(900, 4500),
            (coords,),
            rows_view,
            gate,
            up,
            down,
        )

    got = swap(products(False))
    pairs = call(
        add_kernel,
        (2,),
        [lead_block(4, HALF, 3 * HID)] * 2,
        lead_block(4, HALF, 3 * HID),
        pltpu.HBM((8, HALF, 3 * HID), BF),
        cost(1, 6000),
        (coords,),
        products(True),
        got,
    )
    sums = lax.psum_scatter(pairs.reshape(8 * HALF, 3 * HID), "z", scatter_dimension=0, tiled=True)
    new_rows = slab_rows(jnp.take(held_before, partner), pairs, pltpu.HBM(sent_shape, BF))
    three, acts = call(
        activation_kernel,
        (1,),
        [whole(HALF, 3 * HID), ANYWHERE],
        (whole(3 * HALF, HID), whole(BUNDLE, HID)),
        (shaped(3 * HALF, HID), shaped(BUNDLE, HID)),
        cost(3, 500),
        (coords,),
        in_hbm(sums),
        in_hbm(new_rows),
    )

    own_acts = lax.all_gather(three, ("z", "core"), tiled=True).reshape(CHUNKS, 3 * HALF, HID)
    pieces = exchange(acts.reshape(32, 8, HID), ("y", "x"))
    picked = call(
        pick_kernel,
        (1,),
        [whole(32, 8, HID)],
        whole(32, 8, HID),
        shaped(32, 8, HID),
        cost(1, 520),
        (partner,),
        pieces,
    )
    moved = exchange(picked, ("y", "x")).reshape(BUNDLE, HID)

    terms = call(
        terms_kernel,
        (2,),
        [
            lead_block(8, 3 * HALF, HID),
            whole(FEAT, HID),
            whole(FEAT, HID),
            whole(FEAT, HID),
        ],
        lead_block(ROWS // 2, 2 * FEAT),
        pltpu.HBM((ROWS, 2 * FEAT), BF),
        cost(1800, 8000),
        (coords,),
        in_hbm(own_acts),
        gate,
        up,
        down,
    )
    new_acts = lax.all_gather(moved[: 3 * HALF], ("z", "core"), tiled=True).reshape(CHUNKS, 3 * HALF, HID)

    plain, weighted = call(
        slots_kernel,
        (1,),
        [whole(8, TOK), whole(8, TOK)],
        (whole(TOK, ROWS), whole(TOK, ROWS)),
        (shaped(TOK, ROWS), shaped(TOK, ROWS)),
        cost(20, 400),
        (held_before,),
        ids,
        probs,
    )
    layer_out, token_grad = local(
        merge_kernel,
        (shaped(TOK, FEAT), shaped(TOK, FEAT)),
        cost(300, 2400),
        plain,
        weighted,
        exchange(terms.reshape(32, CAP, 2 * FEAT), ("x", "y")).reshape(ROWS, 2 * FEAT),
    )

    gate_grad, up_grad, down_grad = local(
        slab_grad_kernel,
        (shaped(FEAT, HID), shaped(FEAT, HID), shaped(FEAT, HID)),
        cost(1800, 8000),
        in_hbm(new_rows.reshape(ROWS, 2 * FEAT)),
        in_hbm(new_acts),
    )

    return (layer_out, token_grad, gate_grad[None], up_grad[None], down_grad.T[None])


def solution(mesh):
    fine = Mesh(mesh.devices.reshape(8, 4, 8, 2), ("y", "x", "z", "core"))
    expert, dp = ("y", "x"), ("z", "core")
    slab = P(expert, dp, None)
    down = P(expert, None, dp)
    return jax.shard_map(
        body,
        mesh=fine,
        in_specs=(P(expert, dp), P(expert, dp), P(expert, None), P(expert, None), P(), P(), slab, slab, down),
        out_specs=(P(expert, dp), P(expert, dp), slab, slab, down),
        check_vma=False,
    )
```
